256 devices in a mesh: seq: 4 (over y_lo, core), grp: 8 (over z), head: 8 (over x, y_hi).
Axes of the slice: x: 4, y: 4 (y_hi: 2, y_lo: 2; y = y_hi * 2 + y_lo), z: 8, core: 2. Of those that a mesh axis runs over, the one named last changes fastest.
Arguments:
- queries: bfloat16 [8, 512, 8192], P('grp', 'seq', 'head'), may hold values from -6 to 6
- key_heads: bfloat16 [8, 512, 1024], P('grp', 'seq', 'head'), may hold values from -6 to 6
- value_heads: bfloat16 [8, 512, 1024], P('grp', 'seq', 'head'), may hold values from -6 to 6
- cotangent: bfloat16 [8, 512, 8192], P('grp', 'seq', 'head'), may hold values from -6 to 6
- loss_mask: int32 [8, 512], P('grp', 'seq'), may hold values 0 or 1
- log_ratio: float32 [8, 512], P('grp', ('seq', 'head')), may hold values from -6 to 6
- block_counts: int32 [8], replicated, may hold values from 1 to 2, as said below
- response_order: int32 [8], replicated, may hold values from 0 to 7, each once
Outputs:
- attended: bfloat16 [8, 512, 8192], P('grp', 'seq', 'head')
- query_grad: bfloat16 [8, 512, 8192], P('grp', 'seq', 'head')
- key_grad: bfloat16 [8, 512, 1024], P('grp', 'seq', 'head')
- value_grad: bfloat16 [8, 512, 1024], P('grp', 'seq', 'head')
- pair_loss: float32 [4], replicated
The draws below stay inside these ranges and needn't reach their ends.
Inputs may be any that keep to these rules, and one draw needn't show every extreme that they name: Response slot i holds 128 * block_counts[i] tokens at its start; the rest of its 256 rows is padding. Some slot holds a full response and some slot a single block. Slot i, slot i % 2 of response group 4 + i // 2, holds the chosen response of pair response_order[i] // 2 if the number is even, the rejected one if it is odd.
All inputs are finite; a program needn't handle non-finite values. No bound on the sum of `loss_mask` on one device may be relied on, other than what follows from the above.
Results may differ from the reference program's by a relative error of at most 0.033.
Values may be sent and summed in bfloat16 or wider, within the bound.
No kernel may reach another device: no remote copies, remote signals or barrier semaphores. Data moves between devices by JAX's collectives and lax.ppermute only.
A program may use at most 64 MiB of HBM per device.

```python
import math
import jax
import jax.numpy as jnp
from jax import lax

HEAD_DIM = 128
GROUP_SIZE = 8
LEN_BLOCK = 128
KV_HEADS = 8
Q_HEADS = 64
GROUPS = 8
PAIRS = 4
GROUP_TOK = 512
RESP_LEN = 256


def draw_queries(key, part):
    key = jax.random.fold_in(key, 11)
    shape = (GROUPS, GROUP_TOK, Q_HEADS * HEAD_DIM)
    base = jnp.clip(jax.random.normal(key, shape, jnp.float32), -6.0, 6.0)
    return base.astype(jnp.bfloat16)


def draw_key_heads(key, part):
    key = jax.random.fold_in(key, 17)
    shape = (GROUPS, GROUP_TOK, KV_HEADS * HEAD_DIM)
    base = jnp.clip(jax.random.normal(key, shape, jnp.float32), -6.0, 6.0)
    return base.astype(jnp.bfloat16)


def draw_log_ratio(key, part):
    key = jax.random.fold_in(key, 29)
    rising = 1.0 + 2.0 * jnp.arange(GROUP_TOK, dtype=jnp.float32) / GROUP_TOK
    noise = 0.5 * jnp.clip(jax.random.normal(key, (GROUPS, GROUP_TOK), jnp.float32), -4.0, 4.0)
    return (noise * rising[None, :]).astype(jnp.float32)


def draw_block_counts(key, part):
    key = jax.random.fold_in(key, 41)
    first_key, second_key, third_key = jax.random.split(key, 3)
    most = RESP_LEN // LEN_BLOCK
    counts = jax.random.randint(first_key, (GROUPS,), 1, most + 1)
    full_spot = jax.random.randint(second_key, (), 0, GROUPS)
    short_spot = (full_spot + 1 + jax.random.randint(third_key, (), 0, GROUPS - 1)) % GROUPS
    slots = jnp.arange(GROUPS)
    counts = jnp.where(slots == full_spot, most, counts)
    counts = jnp.where(slots == short_spot, 1, counts)
    return counts.astype(jnp.int32)


def plant(drawn, stream_key, low, high):
    spot = [jax.random.randint(jax.random.fold_in(stream_key, axis), (), 0, length) for axis, length in enumerate(drawn.shape)]
    widest = drawn.shape.index(max(drawn.shape))
    next_to = spot[:widest] + [(spot[widest] + 1) % drawn.shape[widest]] + spot[widest + 1:]
    return drawn.at[tuple(spot)].set(low).at[tuple(next_to)].set(high)


def shard_levels(own_key, dims, cuts, smallest, top_value):
    def one(dim, blocks):
        draws = jax.random.uniform(jax.random.fold_in(jax.random.fold_in(own_key, 6), dim), (blocks,), jnp.float32, smallest / len(cuts), top_value / len(cuts))
        return jnp.repeat(jnp.exp(draws), dims[dim] // blocks).reshape((-1,) + (1,) * (len(dims) - dim - 1))

    factor_of = one(*cuts[0])
    for cut in cuts[1:]:
        factor_of = factor_of * one(*cut)
    return factor_of


def normal_values(stream_key, dims, spread, bound, pieces=(), held_as=jnp.bfloat16):
    level = shard_levels(stream_key, dims, pieces, -0.22, 0.18) if pieces else 1.0
    values = jax.random.normal(stream_key, dims, jnp.float32) * spread * level
    return jnp.minimum(jnp.maximum(values, -bound), bound).astype(held_as)


def setup_inputs(seed: int = 0) -> dict:
    arg_keys = jax.random.split(jax.random.key(seed), 9)
    return {
        "queries": draw_queries(jax.random.fold_in(arg_keys[8], 71), 0),
        "key_heads": draw_key_heads(jax.random.fold_in(arg_keys[8], 71), 0),
        "value_heads": normal_values(arg_keys[2], (GROUPS, GROUP_TOK, KV_HEADS * HEAD_DIM), 1.0, 6.0, ((0, 8), (1, 4), (2, 8))),
        "cotangent": normal_values(arg_keys[3], (GROUPS, GROUP_TOK, Q_HEADS * HEAD_DIM), 1.0, 6.0, ((0, 8), (1, 4), (2, 8))),
        "loss_mask": plant((jax.random.randint(arg_keys[4], (GROUPS, GROUP_TOK), 0, 4) < 3).astype(jnp.int32), jax.random.fold_in(arg_keys[4], 1), 0, 1),
        "log_ratio": draw_log_ratio(jax.random.fold_in(arg_keys[8], 71), 0),
        "block_counts": draw_block_counts(jax.random.fold_in(arg_keys[8], 71), 0),
        "response_order": jax.random.permutation(arg_keys[7], GROUPS).astype(jnp.int32),
    }


BETA = 0.1

def attend(query_block, key_rows, value_rows, grad_block, allowed):
    scaling = 1.0 / math.sqrt(query_block.shape[-1])
    query_wide = query_block.astype(jnp.float32)
    key_wide = key_rows.astype(jnp.float32)
    value_wide = value_rows.astype(jnp.float32)
    grad_wide = grad_block.astype(jnp.float32)
    scores = jnp.einsum('rgd,sd->rgs', query_wide, key_wide) * scaling
    scores = jnp.where(allowed[:, None, :], scores, -jnp.inf)
    running_top = lax.optimization_barrier(jnp.max(scores, axis=-1, keepdims=True))
    weights = jnp.exp(scores - running_top)
    weights = weights / lax.optimization_barrier(jnp.sum(weights, axis=-1, keepdims=True))
    rounded = lax.optimization_barrier(weights.astype(jnp.bfloat16)).astype(jnp.float32)
    output = jnp.einsum('rgs,sd->rgd', rounded, value_wide)
    prob_grad = jnp.einsum('rgd,sd->rgs', grad_wide, value_wide)
    row_delta = lax.optimization_barrier(jnp.sum(grad_wide * output, axis=-1, keepdims=True))
    score_grad = lax.optimization_barrier((weights * (prob_grad - row_delta) * scaling).astype(jnp.bfloat16)).astype(jnp.float32)
    query_part = jnp.einsum('rgs,sd->rgd', score_grad, key_wide)
    key_part = jnp.einsum('rgs,rgd->sd', score_grad, query_wide)
    value_part = jnp.einsum('rgs,rgd->sd', rounded, grad_wide)
    return (output, query_part, key_part, value_part)

def by_heads(query_rows, key_rows, value_rows, grad_rows, allowed):
    row_total = query_rows.shape[0]
    key_total = key_rows.shape[0]
    query_split = query_rows.reshape(row_total, KV_HEADS, GROUP_SIZE, HEAD_DIM).transpose(1, 0, 2, 3)
    grad_split = grad_rows.reshape(row_total, KV_HEADS, GROUP_SIZE, HEAD_DIM).transpose(1, 0, 2, 3)
    key_split = key_rows.reshape(key_total, KV_HEADS, HEAD_DIM).transpose(1, 0, 2)
    value_split = value_rows.reshape(key_total, KV_HEADS, HEAD_DIM).transpose(1, 0, 2)

    def one_head(items):
        return attend(items[0], items[1], items[2], items[3], allowed)
    output, query_part, key_part, value_part = lax.map(one_head, (query_split, key_split, value_split, grad_split))
    output = output.transpose(1, 0, 2, 3).reshape(row_total, -1)
    query_part = query_part.transpose(1, 0, 2, 3).reshape(row_total, -1)
    key_part = key_part.transpose(1, 0, 2).reshape(key_total, -1)
    value_part = value_part.transpose(1, 0, 2).reshape(key_total, -1)
    return (output, query_part, key_part, value_part)

def reference(queries, key_heads, value_heads, cotangent, loss_mask, log_ratio, block_counts, response_order):
    row_ids = jnp.arange(GROUP_TOK)
    slot_of_row = row_ids // RESP_LEN
    position = row_ids % RESP_LEN
    group_ids = jnp.arange(GROUPS)
    is_response = group_ids[:, None] >= PAIRS
    safe_slot = jnp.clip(2 * (group_ids[:, None] - PAIRS) + slot_of_row[None, :], 0, GROUPS - 1)
    lengths = block_counts * LEN_BLOCK
    is_valid = jnp.logical_or(jnp.logical_not(is_response), position[None, :] < lengths[safe_slot])
    is_kept = jnp.logical_and(is_valid, loss_mask > 0)
    ratio_terms = jnp.where(is_kept, log_ratio, jnp.zeros((), jnp.float32))
    slot_totals = lax.optimization_barrier(jnp.sum(ratio_terms[PAIRS:].reshape(PAIRS, 2, RESP_LEN), axis=-1)).reshape(GROUPS)
    totals = jnp.zeros((GROUPS,), jnp.float32).at[response_order].set(slot_totals)
    margin = totals[0::2] - totals[1::2]
    pair_loss = jnp.logaddexp(jnp.zeros((), jnp.float32), -BETA * margin)
    weight = jax.nn.sigmoid(-BETA * margin)
    response_id = response_order[safe_slot]
    signed = jnp.where(response_id % 2 == 0, -1.0, 1.0) * weight[response_id // 2]
    prompt_weight = weight[jnp.clip(group_ids, 0, PAIRS - 1)][:, None]
    coefficient = jnp.where(is_response, signed, prompt_weight)
    coefficient = jnp.where(is_kept, coefficient, jnp.zeros((), jnp.float32))
    grad_rows = (coefficient[:, :, None] * cotangent.astype(jnp.float32)).astype(jnp.bfloat16)
    causal_group = row_ids[None, :] <= row_ids[:, None]
    causal_slot = position[None, :RESP_LEN] <= position[:RESP_LEN, None]
    response_allowed = jnp.concatenate([jnp.ones((RESP_LEN, GROUP_TOK), bool), causal_slot], axis=1)
    key_total = jnp.zeros((GROUPS, GROUP_TOK, KV_HEADS * HEAD_DIM), jnp.float32)
    value_total = jnp.zeros((GROUPS, GROUP_TOK, KV_HEADS * HEAD_DIM), jnp.float32)
    outputs = []
    query_grads = []
    for group_id in range(PAIRS):
        output, query_part, key_part, value_part = by_heads(queries[group_id], key_heads[group_id], value_heads[group_id], grad_rows[group_id], causal_group)
        outputs.append(output)
        query_grads.append(query_part)
        key_total = key_total.at[group_id].add(key_part)
        value_total = value_total.at[group_id].add(value_part)
    for group_id in range(PAIRS, GROUPS):
        group_out = []
        group_query = []
        for slot_number in range(2):
            row_start = slot_number * RESP_LEN
            prompt = response_order[2 * (group_id - PAIRS) + slot_number] // 2
            key_rows = jnp.concatenate([key_heads[prompt], key_heads[group_id, row_start:row_start + RESP_LEN]], axis=0)
            value_rows = jnp.concatenate([value_heads[prompt], value_heads[group_id, row_start:row_start + RESP_LEN]], axis=0)
            output, query_part, key_part, value_part = by_heads(queries[group_id, row_start:row_start + RESP_LEN], key_rows, value_rows, grad_rows[group_id, row_start:row_start + RESP_LEN], response_allowed)
            group_out.append(output)
            group_query.append(query_part)
            key_total = key_total.at[prompt].add(key_part[:GROUP_TOK])
            value_total = value_total.at[prompt].add(value_part[:GROUP_TOK])
            key_total = key_total.at[group_id, row_start:row_start + RESP_LEN].add(key_part[GROUP_TOK:])
            value_total = value_total.at[group_id, row_start:row_start + RESP_LEN].add(value_part[GROUP_TOK:])
        outputs.append(jnp.concatenate(group_out, axis=0))
        query_grads.append(jnp.concatenate(group_query, axis=0))
    output_all = jnp.stack(outputs)
    attended = jnp.where(is_valid[:, :, None], output_all, jnp.zeros((), jnp.float32)).astype(jnp.bfloat16)
    query_grad = jnp.stack(query_grads).astype(jnp.bfloat16)
    return (attended, query_grad, key_total.astype(jnp.bfloat16), value_total.astype(jnp.bfloat16), pair_loss)
```

```python
import functools
import math

import jax
import jax.numpy as jnp
from jax import lax
from jax.experimental import pallas as pl
from jax.experimental.pallas import tpu as pltpu
from jax.sharding import PartitionSpec as P

LEN_BLOCK = 128
BETA = 0.1
NEG_FILL = -1e30
LOG2_E = math.log2(math.e)
TAIL = 16
F32 = jnp.float32
BF16 = jnp.bfloat16
VMEM_BYTES = 40 * 1024 * 1024

SMEM_SPEC = pl.BlockSpec(memory_space=pltpu.SMEM)
VMEM_SPEC = pl.BlockSpec(memory_space=pltpu.VMEM)


def dot(lhs, rhs, lhs_dim, rhs_dim):
    return lax.dot_general(
        lhs, rhs, (((lhs_dim,), (rhs_dim,)), ((), ())), preferred_element_type=F32
    )


def place():
    seq = lax.axis_index("seq")
    grp = lax.axis_index("grp")
    pairs = lax.axis_size("grp") // 2
    is_response = grp >= pairs
    first_slot = jnp.where(is_response, 2 * (grp - pairs), 0)
    return seq, grp, pairs, is_response, first_slot


def encode(totals):
    high = totals.astype(BF16).astype(F32)
    rest = totals - high
    middle = rest.astype(BF16).astype(F32)
    low = rest - middle
    left = jnp.concatenate([high, low], axis=0).astype(BF16)
    right = jnp.concatenate([middle, jnp.zeros_like(middle)], axis=0).astype(BF16)
    return left, right


def decode(ref, row):
    left = ref[row : row + TAIL, :128].astype(F32)
    right = ref[row : row + TAIL, 128:].astype(F32)
    return (left[:8] + right[:8]) + left[8:]


def store_tail(ref, row, totals):
    left, right = encode(totals)
    ref[row : row + TAIL, :128] = left
    ref[row : row + TAIL, 128:] = right


def pack_kernel(order_ref, counts_ref, key_ref, value_ref, mask_ref, ratio_ref, out_ref):
    seq, grp, pairs, is_response, first_slot = place()
    head = lax.axis_index("head")
    rows, dim = key_ref.shape
    piece = ratio_ref.shape[1]
    slot = first_slot + seq // 2
    valid = jnp.logical_and(is_response, seq % 2 < counts_ref[slot])
    lane = lax.broadcasted_iota(jnp.int32, (piece, 128), 1)
    spot = lax.broadcasted_iota(jnp.int32, (piece, 128), 0)
    place_at = (lane == spot + head * piece).astype(F32)
    spread = lax.dot_general(
        jnp.broadcast_to(ratio_ref[...], (8, piece)),
        place_at,
        (((1,), (0,)), ((), ())),
        precision=lax.Precision.HIGHEST,
        preferred_element_type=F32,
    )
    kept = mask_ref[...] > 0
    partial = jnp.sum(jnp.where(kept, spread[:1], 0.0), axis=1, keepdims=True)
    row = lax.broadcasted_iota(jnp.int32, (8, 128), 0)
    mine = jnp.where(valid, order_ref[slot], -1)
    totals = jnp.where(row == mine, jnp.broadcast_to(partial, (8, 128)), 0.0)
    out_ref[:rows, :dim] = key_ref[...]
    out_ref[:rows, dim:] = value_ref[...]
    store_tail(out_ref, rows, totals)


def route_kernel(order_ref, own_ref, far4, far5, far6, far7, near_ref, other_ref):
    seq, grp, pairs, is_response, first_slot = place()
    rows = own_ref.shape[0] - TAIL
    far = ((4, far4), (5, far5), (6, far6), (7, far7))
    own_pair = order_ref[first_slot + seq // 2] // 2
    other_pair = order_ref[first_slot + 1 - seq // 2] // 2
    near_ref[rows : 2 * rows] = own_ref[:rows]

    @pl.when(jnp.logical_not(is_response))
    def _():
        near_ref[:rows] = own_ref[:rows]
        other_ref[:rows] = own_ref[:rows]

    for turn, ref in far:
        source = grp ^ turn

        @pl.when(jnp.logical_and(is_response, own_pair == source))
        def _():
            near_ref[:rows] = ref[:rows]

        @pl.when(jnp.logical_and(is_response, other_pair == source))
        def _():
            other_ref[:rows] = ref[:rows]

    totals = (decode(far4, rows) + decode(far5, rows)) + (decode(far6, rows) + decode(far7, rows))
    store_tail(near_ref, 2 * rows, totals)
    store_tail(other_ref, rows, totals)


def totals_kernel(near_ref, seq1, seq2, seq3, out_ref):
    rows = seq2.shape[0] - TAIL
    out_ref[...] = (decode(near_ref, 2 * rows) + decode(seq1, 2 * rows)) + (
        decode(seq2, rows) + decode(seq3, rows)
    )


def attend_kernel(
    order_ref,
    counts_ref,
    query_ref,
    cot_ref,
    mask_ref,
    near_ref,
    seq1,
    seq2,
    seq3,
    attended_ref,
    query_grad_ref,
    back1,
    back2,
    back3,
    first_ref,
    own_ref,
    keys,
    values,
    keys_t,
    values_t,
    key_acc,
    value_acc,
):
    seq, grp, pairs, is_response, first_slot = place()
    rows = mask_ref.shape[1]
    dim = keys.shape[1]
    heads = query_ref.shape[1] // dim
    scaling = 1.0 / math.sqrt(dim)
    slot = first_slot + seq // 2
    valid = jnp.logical_or(jnp.logical_not(is_response), seq % 2 < counts_ref[slot])
    negative = jnp.logical_and(is_response, order_ref[slot] % 2 == 0)
    sign = jnp.where(valid, jnp.where(negative, -1.0, 1.0), 0.0).astype(F32)

    blocks = (
        (near_ref, 0),
        (seq1, 0),
        (seq2, 0),
        (seq3, 0),
        (seq1, rows),
        (near_ref, rows),
    )
    for number, (ref, start) in enumerate(blocks):
        part = slice(number * rows, (number + 1) * rows)
        key_part = ref[start : start + rows, :dim]
        value_part = ref[start : start + rows, dim:]
        keys[part] = key_part
        values[part] = value_part
        keys_t[:, part] = key_part.T
        values_t[:, part] = value_part.T

    open_blocks = [is_response]
    for turn in (1, 2, 3):
        open_blocks.append(jnp.logical_or(is_response, (seq ^ turn) < seq))
    open_blocks.append(jnp.logical_and(is_response, seq % 2 == 1))
    bias = [jnp.where(is_open, 0.0, NEG_FILL).astype(F32) for is_open in open_blocks]

    wide = 2 * rows
    key_id = lax.broadcasted_iota(jnp.int32, (rows, wide), 0)
    row_id = lax.broadcasted_iota(jnp.int32, (rows, wide), 1) % rows
    causal = key_id <= row_id
    kept = jnp.where(mask_ref[...] > 0, sign, 0.0)
    kept_rows = jnp.broadcast_to(kept, (rows, rows)).T
    shade = LOG2_E * scaling
    last = len(blocks) - 1

    for pair in range(heads // 2):
        spans = [slice((2 * pair + i) * dim, (2 * pair + i + 1) * dim) for i in (0, 1)]
        query = jnp.concatenate([query_ref[:, span] for span in spans], axis=0)
        grad = jnp.concatenate(
            [(cot_ref[:, span].astype(F32) * kept_rows).astype(BF16) for span in spans], axis=0
        )
        scores = dot(keys[...], query, 1, 1)
        pieces = [scores[i * rows : (i + 1) * rows] for i in range(last)]
        pieces.append(jnp.where(causal, scores[last * rows :], NEG_FILL))
        top = jnp.max(pieces[last], axis=0, keepdims=True)
        for i in range(last):
            top = jnp.maximum(top, jnp.max(pieces[i], axis=0, keepdims=True) + bias[i])
        shift = -shade * top
        powers = []
        total = jnp.zeros_like(top)
        for i in range(last + 1):
            lift = shift if i == last else shift + bias[i]
            power = jnp.exp2(pieces[i] * shade + lift)
            total = total + jnp.sum(power, axis=0, keepdims=True)
            powers.append(power)
        inverse = 1.0 / total
        probs = jnp.concatenate(powers, axis=0) * inverse
        rounded = probs.astype(BF16)
        output_t = dot(values_t[...], rounded, 1, 0)
        grad_t = grad.astype(F32).T
        delta = jnp.sum(grad_t * output_t, axis=0, keepdims=True)
        prob_grad = dot(values[...], grad, 1, 1)
        score_grad = (probs * (prob_grad - delta)).astype(BF16)
        query_grad_t = dot(keys_t[...], score_grad, 1, 0) * scaling
        key_part = dot(score_grad, query, 1, 0)
        value_part = dot(rounded, grad, 1, 0)
        if pair == 0:
            key_acc[...] = key_part
            value_acc[...] = value_part
        else:
            key_acc[...] += key_part
            value_acc[...] += value_part
        output = jnp.where(valid, output_t, 0.0).T
        query_grad = query_grad_t.T
        for i, span in enumerate(spans):
            part = slice(i * rows, (i + 1) * rows)
            attended_ref[:, span] = output[part].astype(BF16)
            query_grad_ref[:, span] = query_grad[part]

    def block(number):
        part = slice(number * rows, (number + 1) * rows)
        return key_acc[part] * scaling, value_acc[part]

    for number, ref, start in (
        (0, first_ref, 0),
        (1, back1, 0),
        (2, back2, 0),
        (3, back3, 0),
        (4, back1, rows),
        (5, own_ref, 0),
    ):
        key_part, value_part = block(number)
        ref[start : start + rows, :dim] = key_part.astype(ref.dtype)
        ref[start : start + rows, dim:] = value_part.astype(ref.dtype)


def return_kernel(
    order_ref, first_ref, own_ref, back1, back2, back3, totals_ref, local_ref, *pay_refs
):
    seq, grp, pairs, is_response, first_slot = place()
    rows = first_ref.shape[0]
    own_pair = order_ref[first_slot + seq // 2] // 2
    other_pair = order_ref[first_slot + 1 - seq // 2] // 2
    mate = back1[:rows].astype(F32)
    across = back2[...].astype(F32) + back3[...].astype(F32)
    as_prompt = jnp.where(is_response, 0.0, 1.0).astype(F32)
    local_ref[...] = own_ref[...] + back1[rows:].astype(F32) + (mate + across) * as_prompt
    own_sum = first_ref[...] + mate
    none = jnp.zeros((8, 128), F32)
    for turn, ref in zip((4, 5, 6, 7), pay_refs):
        target = grp ^ turn
        take_own = jnp.logical_and(is_response, own_pair == target)
        take_other = jnp.logical_and(is_response, other_pair == target)
        own_factor = jnp.where(take_own, 1.0, 0.0).astype(F32)
        other_factor = jnp.where(take_other, 1.0, 0.0).astype(F32)
        ref[:rows] = (own_sum * own_factor + across * other_factor).astype(BF16)
        store_tail(ref, rows, none if turn == 4 else totals_ref[...])


def add_kernel(left_ref, right_ref, out_ref):
    out_ref[...] = (left_ref[...].astype(F32) + right_ref[...].astype(F32)).astype(BF16)


def finish_kernel(
    order_ref,
    local_ref,
    far5,
    far6,
    far7,
    totals_ref,
    query_part_ref,
    query_grad_ref,
    key_grad_ref,
    value_grad_ref,
    loss_ref,
):
    seq, grp, pairs, is_response, first_slot = place()
    rows, dim = key_grad_ref.shape
    totals = totals_ref[...] + decode(far7, rows)
    margin = totals - jnp.concatenate([totals[1:], totals[:1]], axis=0)
    slope = -BETA * margin
    small = jnp.exp(-jnp.abs(slope))
    bigger = 1.0 + small
    gap = bigger - 1.0
    log_part = jnp.where(
        gap == 0.0, small, jnp.log(bigger) * (small / jnp.where(gap == 0.0, 1.0, gap))
    )
    loss = jnp.maximum(slope, 0.0) + log_part
    weight = jnp.where(slope >= 0.0, 1.0, small) / bigger
    row = lax.broadcasted_iota(jnp.int32, (8, 128), 0)
    lane = lax.broadcasted_iota(jnp.int32, (8, 128), 1)
    in_lanes = jnp.sum(jnp.where(row == 2 * lane, loss, 0.0), axis=0, keepdims=True)
    loss_ref[...] = in_lanes[:, : loss_ref.shape[1]]
    own_pair = order_ref[first_slot + seq // 2] // 2
    my_pair = jnp.where(is_response, own_pair, jnp.minimum(grp, pairs - 1))
    scale = jnp.sum(jnp.where(row == 2 * my_pair, weight, 0.0), axis=0, keepdims=True)
    as_prompt = jnp.where(is_response, 0.0, 1.0).astype(F32)
    far_sum = far5[:rows].astype(F32) + far6[:rows].astype(F32) + far7[:rows].astype(F32)
    total = local_ref[...] + far_sum * as_prompt
    key_grad_ref[...] = (total[:, :dim] * scale).astype(BF16)
    value_grad_ref[...] = (total[:, dim:] * scale).astype(BF16)
    for start in range(0, query_grad_ref.shape[1], dim):
        span = slice(start, start + dim)
        query_grad_ref[:, span] = (query_part_ref[:, span] * scale).astype(BF16)


def call(kernel, out_shapes, in_specs, scratch=(), flops=0, bytes_accessed=0):
    single = not isinstance(out_shapes, (list, tuple))
    return pl.pallas_call(
        kernel,
        out_shape=out_shapes,
        in_specs=in_specs,
        out_specs=VMEM_SPEC if single else [VMEM_SPEC] * len(out_shapes),
        scratch_shapes=list(scratch),
        compiler_params=pltpu.CompilerParams(vmem_limit_bytes=VMEM_BYTES),
        cost_estimate=pl.CostEstimate(
            flops=flops, bytes_accessed=bytes_accessed, transcendentals=0
        ),
    )


def swap(count, turn):
    return [(i, i ^ turn) for i in range(count)]


def body(
    queries, key_heads, value_heads, cotangent, loss_mask, log_ratio, block_counts, response_order
):
    seq_count = lax.axis_size("seq")
    group_count = lax.axis_size("grp")
    head_count = lax.axis_size("head")
    rows = queries.shape[1]
    dim = key_heads.shape[2]
    width = queries.shape[2]
    pair_width = 2 * dim
    blocks = seq_count + 2
    shape = jax.ShapeDtypeStruct
    packed = shape((rows + TAIL, pair_width), BF16)
    total_tile = shape((8, 128), F32)

    def along_grp(value, turn):
        return lax.ppermute(value, "grp", swap(group_count, turn))

    def along_seq(value, turn):
        return lax.ppermute(value, "seq", swap(seq_count, turn))

    own = call(pack_kernel, packed, [SMEM_SPEC] * 2 + [VMEM_SPEC] * 4)(
        response_order, block_counts, key_heads[0], value_heads[0], loss_mask, log_ratio
    )
    far5 = along_grp(own, 5)
    far6 = along_grp(own, 6)
    far7 = along_grp(own, 7)
    far4 = along_grp(far5, 1)
    near, other = call(
        route_kernel,
        [shape((2 * rows + TAIL, pair_width), BF16), packed],
        [SMEM_SPEC] + [VMEM_SPEC] * 5,
    )(response_order, own, far4, far5, far6, far7)
    seq1 = along_seq(near, 1)
    seq2 = along_seq(other, 2)
    seq3 = along_seq(other, 3)
    totals = call(totals_kernel, total_tile, [VMEM_SPEC] * 4)(near, seq1, seq2, seq3)
    half = head_count // 2
    turn_x1 = [(h, h ^ 2) for h in range(head_count)]
    turn_x2 = [(h, (3 - h // 2) * 2 + h % 2) for h in range(head_count)]
    turn_y = [
        (s * head_count + h, (s ^ 2) * head_count + (h ^ 1))
        for s in range(seq_count)
        for h in range(head_count)
    ]
    totals = totals + lax.ppermute(totals, "head", turn_x1)
    totals = totals + lax.ppermute(totals, "head", turn_x2)
    totals = totals + lax.ppermute(totals, ("seq", "head"), turn_y)

    grads = shape((rows, pair_width), BF16)
    grads_wide = shape((rows, pair_width), F32)
    attended, query_part, back1, back2, back3, first, local = call(
        attend_kernel,
        [
            shape((rows, width), BF16),
            shape((rows, width), F32),
            shape((2 * rows, pair_width), BF16),
            grads,
            grads,
            grads_wide,
            grads_wide,
        ],
        [SMEM_SPEC] * 2 + [VMEM_SPEC] * 7,
        scratch=[
            pltpu.VMEM((blocks * rows, dim), BF16),
            pltpu.VMEM((blocks * rows, dim), BF16),
            pltpu.VMEM((dim, blocks * rows), BF16),
            pltpu.VMEM((dim, blocks * rows), BF16),
            pltpu.VMEM((blocks * rows, dim), F32),
            pltpu.VMEM((blocks * rows, dim), F32),
        ],
        flops=12 * rows * width * blocks * rows,
        bytes_accessed=6 * rows * width * 2,
    )(
        response_order,
        block_counts,
        queries[0],
        cotangent[0],
        loss_mask,
        near,
        seq1,
        seq2,
        seq3,
    )
    back1 = along_seq(back1, 1)
    back2 = along_seq(back2, 2)
    back3 = along_seq(back3, 3)
    local, pay4, pay5, pay6, pay7 = call(
        return_kernel, [grads_wide] + [packed] * 4, [SMEM_SPEC] + [VMEM_SPEC] * 6
    )(response_order, first, local, back1, back2, back3, totals)
    pay4 = along_grp(pay4, 1)
    pay5 = call(add_kernel, packed, [VMEM_SPEC] * 2)(pay5, pay4)
    far7 = along_grp(pay7, 7)
    far6 = along_grp(pay6, 6)
    far5 = along_grp(pay5, 5)
    query_grad, key_grad, value_grad, loss = call(
        finish_kernel,
        [
            shape((rows, width), BF16),
            shape((rows, dim), BF16),
            shape((rows, dim), BF16),
            shape((1, group_count // 2), F32),
        ],
        [SMEM_SPEC] + [VMEM_SPEC] * 6,
    )(response_order, local, far5, far6, far7, totals, query_part)
    return attended[None], query_grad[None], key_grad[None], value_grad[None], loss[0]


def solution(mesh):
    spec = P("grp", "seq", "head")
    in_specs = (spec, spec, spec, spec, P("grp", "seq"), P("grp", ("seq", "head")), P(), P())
    out_specs = (spec, spec, spec, spec, P())
    return jax.shard_map(body, mesh=mesh, in_specs=in_specs, out_specs=out_specs, check_vma=False)
```

```python
import functools
import math

import jax
import jax.numpy as jnp
from jax import lax
from jax.experimental import pallas as pl
from jax.experimental.pallas import tpu as pltpu
from jax.sharding import PartitionSpec as P

LEN_BLOCK = 128
BETA = 0.1
NEG_FILL = -1e30
LOG2_E = math.log2(math.e)
TAIL = 16
F32 = jnp.float32
BF16 = jnp.bfloat16
VMEM_BYTES = 40 * 1024 * 1024

VMEM_SPEC = pl.BlockSpec(memory_space=pltpu.VMEM)
HBM_SPEC = pl.BlockSpec(memory_space=pltpu.HBM)

FROM7, FROM5, IS_PROMPT, VALID, PAIR_ROW = 0, 4, 8, 9, 10
BIAS_FIRST, BIAS_MATE, BIAS_OVER, BIAS_CROSS, BIAS_OWN = 11, 12, 13, 14, 15
FACTS = 16


def dot(lhs, rhs, lhs_dim, rhs_dim):
    return lax.dot_general(
        lhs, rhs, (((lhs_dim,), (rhs_dim,)), ((), ())), preferred_element_type=F32
    )


def fact(facts_ref, row, width=None):
    return facts_ref[row : row + 1, :width]


def store_tail(ref, row, totals):
    high = totals.astype(BF16).astype(F32)
    rest = totals - high
    middle = rest.astype(BF16).astype(F32)
    low = rest - middle
    zero = jnp.zeros_like(middle)
    ref[row : row + TAIL, :128] = jnp.concatenate([high, low], axis=0).astype(BF16)
    ref[row : row + TAIL, 128:] = jnp.concatenate([middle, zero], axis=0).astype(BF16)


def decode(ref, row):
    left = ref[row : row + TAIL, :128].astype(F32)
    right = ref[row : row + TAIL, 128:].astype(F32)
    return (left[:8] + right[:8]) + left[8:]


def pack_kernel(key_ref, value_ref, out_ref, sems):
    dim = key_ref.shape[1]
    copies = [
        pltpu.make_async_copy(ref, out_ref.at[:, pl.ds(i * dim, dim)], sems.at[i])
        for i, ref in enumerate((key_ref, value_ref))
    ]
    for copy in copies:
        copy.start()
    for copy in copies:
        copy.wait()


def facts_kernel(
    order_hbm,
    counts_hbm,
    mask_hbm,
    ratio_hbm,
    facts_ref,
    totals_ref,
    kept_ref,
    order_ref,
    counts_ref,
    mask_ref,
    ratio_ref,
    sems,
):
    copies = [
        pltpu.make_async_copy(source, target, sems.at[i])
        for i, (source, target) in enumerate(
            (
                (order_hbm, order_ref),
                (counts_hbm, counts_ref),
                (mask_hbm, mask_ref),
                (ratio_hbm, ratio_ref),
            )
        )
    ]
    for copy in copies:
        copy.start()
    seq = lax.axis_index("seq")
    grp = lax.axis_index("grp")
    head = lax.axis_index("head")
    pairs = lax.axis_size("grp") // 2
    is_response = grp >= pairs
    for copy in copies:
        copy.wait()

    def pair_of(group, half):
        return order_ref[jnp.where(is_response, 2 * (group - pairs), 0) + half] // 2

    def put(row, value):
        facts_ref[row : row + 1, :] = jnp.full((1, facts_ref.shape[1]), value, F32)

    def flag(row, condition, yes=1.0, no=0.0):
        put(row, jnp.where(condition, yes, no).astype(F32))

    half = seq // 2
    slots = [pair_of(group, side) for side in (half, 1 - half) for group in (grp, grp ^ 1)]
    for number, pair in enumerate(slots):
        flag(FROM7 + number, jnp.logical_and(is_response, pair == (grp ^ 7)))
        flag(FROM5 + number, jnp.logical_and(is_response, pair == (grp ^ 5)))
    slot = jnp.where(is_response, 2 * (grp - pairs), 0) + half
    filled = seq % 2 < counts_ref[slot]
    valid = jnp.logical_or(jnp.logical_not(is_response), filled)
    my_pair = jnp.where(is_response, order_ref[slot] // 2, jnp.minimum(grp, pairs - 1))
    flag(IS_PROMPT, jnp.logical_not(is_response))
    flag(VALID, valid)
    put(PAIR_ROW, (2 * my_pair).astype(F32))
    flag(BIAS_FIRST, is_response, 0.0, NEG_FILL)
    flag(BIAS_MATE, jnp.logical_or(is_response, seq % 2 == 1), 0.0, NEG_FILL)
    flag(BIAS_OVER, jnp.logical_or(is_response, seq >= 2), 0.0, NEG_FILL)
    flag(BIAS_CROSS, jnp.logical_or(is_response, seq >= 2), 0.0, NEG_FILL)
    flag(BIAS_OWN, jnp.logical_and(is_response, seq % 2 == 1), 0.0, NEG_FILL)

    piece = ratio_ref.shape[1]
    lane = lax.broadcasted_iota(jnp.int32, (piece, 128), 1)
    spot = lax.broadcasted_iota(jnp.int32, (piece, 128), 0)
    place_at = (lane == spot + head * piece).astype(F32)
    spread = lax.dot_general(
        jnp.broadcast_to(ratio_ref[...], (8, piece)),
        place_at,
        (((1,), (0,)), ((), ())),
        precision=lax.Precision.HIGHEST,
        preferred_element_type=F32,
    )
    kept = mask_ref[...] > 0
    partial = jnp.sum(jnp.where(kept, spread[:1], 0.0), axis=1, keepdims=True)
    row = lax.broadcasted_iota(jnp.int32, (8, 128), 0)
    mine = jnp.where(jnp.logical_and(is_response, filled), order_ref[slot], -1)
    totals_ref[...] = jnp.where(row == mine, jnp.broadcast_to(partial, (8, 128)), 0.0)
    negative = jnp.logical_and(is_response, order_ref[slot] % 2 == 0)
    sign = jnp.where(valid, jnp.where(negative, -1.0, 1.0), 0.0).astype(F32)
    kept_ref[...] = jnp.where(kept, sign, 0.0)


def prepare_kernel(kept_ref, query_hbm, cot_hbm, query_ref, grad_ref, grad_t_ref, cots, sems):
    rows = kept_ref.shape[1]
    dim = query_ref.shape[1]
    heads = query_ref.shape[0] // rows
    copies = []
    for i in range(heads):
        for j, (source, target) in enumerate(((cot_hbm, cots), (query_hbm, query_ref))):
            copies.append(
                pltpu.make_async_copy(
                    source.at[:, pl.ds(i * dim, dim)],
                    target.at[pl.ds(i * rows, rows)],
                    sems.at[j, i],
                )
            )
    for copy in copies:
        copy.start()
    kept_rows = jnp.broadcast_to(kept_ref[...], (rows, rows)).T
    for copy in copies:
        copy.wait()
    for i in range(heads):
        part = slice(i * rows, (i + 1) * rows)
        grad = (cots[part].astype(F32) * kept_rows).astype(BF16)
        grad_ref[part] = grad
        grad_t_ref[:, part] = grad.T


def route_kernel(facts_ref, totals_ref, own_ref, far7, far5, group_ref, seq_ref, cross_ref):
    rows = own_ref.shape[0]
    for number, ref in ((1, group_ref), (2, seq_ref), (3, cross_ref)):
        picked = far7[...].astype(F32) * fact(facts_ref, FROM7 + number)
        picked = picked + far5[...].astype(F32) * fact(facts_ref, FROM5 + number)
        if number == 2:
            picked = picked + own_ref[...].astype(F32) * fact(facts_ref, IS_PROMPT)
        ref[:rows] = picked.astype(BF16)
        store_tail(ref, rows, totals_ref[...])


def select_kernel(
    facts_ref, totals_ref, own_ref, far7, far5, group_ref, seq_ref, cross_ref, near_ref, sum_ref
):
    rows = own_ref.shape[0]
    first = far7[...].astype(F32) * fact(facts_ref, FROM7)
    first = first + far5[...].astype(F32) * fact(facts_ref, FROM5)
    first = first + own_ref[...].astype(F32) * fact(facts_ref, IS_PROMPT)
    near_ref[:rows] = (first + group_ref[:rows].astype(F32)).astype(BF16)
    near_ref[rows:] = (seq_ref[:rows].astype(F32) + cross_ref[:rows].astype(F32)).astype(BF16)
    sum_ref[...] = (totals_ref[...] + decode(group_ref, rows)) + (
        decode(seq_ref, rows) + decode(cross_ref, rows)
    )


def load_blocks(blocks, keys, values, keys_t, values_t):
    dim = keys.shape[1]
    rows = keys.shape[0] // len(blocks)
    for number, (ref, start) in enumerate(blocks):
        part = slice(number * rows, (number + 1) * rows)
        key_part = ref[start : start + rows, :dim]
        value_part = ref[start : start + rows, dim:]
        keys[part] = key_part
        values[part] = value_part
        keys_t[:, part] = key_part.T
        values_t[:, part] = value_part.T


def early_kernel(
    biases,
    is_own,
    facts_ref,
    query_ref,
    grad_ref,
    left_ref,
    right_ref,
    powers_ref,
    prob_grad_ref,
    stats_ref,
    keys_t,
    values_t,
    keys,
    values,
):
    rows = keys.shape[0] // 2
    heads = query_ref.shape[0] // rows
    shade = LOG2_E / math.sqrt(keys.shape[1])
    start = 0 if is_own else rows
    load_blocks(((left_ref, 0), (right_ref, start)), keys, values, keys_t, values_t)
    wide = 2 * rows
    key_id = lax.broadcasted_iota(jnp.int32, (rows, wide), 0)
    row_id = lax.broadcasted_iota(jnp.int32, (rows, wide), 1) % rows
    causal = key_id <= row_id
    bias = [fact(facts_ref, row, wide) if row is not None else 0.0 for row in biases]
    for pair in range(heads // 2):
        both = slice(pair * wide, (pair + 1) * wide)
        scores = dot(keys[...], query_ref[both], 1, 1)
        prob_grad_ref[:, both] = dot(values[...], grad_ref[both], 1, 1)
        pieces = [scores[:rows], scores[rows:]]
        if is_own:
            pieces[1] = jnp.where(causal, pieces[1], NEG_FILL)
        tops = [jnp.max(piece, axis=0, keepdims=True) for piece in pieces]
        top = jnp.maximum(tops[0] + bias[0], tops[1] + bias[1])
        total = jnp.zeros_like(top)
        for i, piece in enumerate(pieces):
            power = jnp.exp2(piece * shade + (bias[i] - shade * top))
            total = total + jnp.sum(power, axis=0, keepdims=True)
            powers_ref[i * rows : (i + 1) * rows, both] = power
        stats_ref[0:1, both] = top
        stats_ref[1:2, both] = total


def late_kernel(
    facts_ref,
    query_ref,
    grad_ref,
    grad_t_ref,
    own_powers,
    own_prob_grad,
    own_stats,
    own_values_t,
    near_powers,
    near_prob_grad,
    near_stats,
    near_values_t,
    mate_ref,
    back_ref,
    first_ref,
    over_ref,
    own_ref,
    output_t_ref,
    own_score_grad,
    near_score_grad,
    mate_score_grad,
    keys_t,
    keys,
    values,
    values_t,
    own_key_acc,
    own_value_acc,
    near_key_acc,
    near_value_acc,
    mate_key_acc,
    mate_value_acc,
):
    rows, dim = keys.shape[0] // 2, keys.shape[1]
    heads = query_ref.shape[0] // rows
    scaling = 1.0 / math.sqrt(dim)
    shade = LOG2_E * scaling
    load_blocks(((mate_ref, 0), (mate_ref, rows)), keys, values, keys_t, values_t)
    wide = 2 * rows
    bias = [fact(facts_ref, row, wide) for row in (BIAS_MATE, BIAS_CROSS)]
    for pair in range(heads // 2):
        both = slice(pair * wide, (pair + 1) * wide)
        query = query_ref[both]
        grad = grad_ref[both]
        scores = dot(keys[...], query, 1, 1)
        prob_grad = dot(values[...], grad, 1, 1)
        pieces = [scores[:rows], scores[rows:]]
        tops = [jnp.max(pieces[i], axis=0, keepdims=True) + bias[i] for i in (0, 1)]
        own_top, near_top = own_stats[0:1, both], near_stats[0:1, both]
        top = jnp.maximum(jnp.maximum(own_top, near_top), jnp.maximum(tops[0], tops[1]))
        powers = [jnp.exp2(pieces[i] * shade + (bias[i] - shade * top)) for i in (0, 1)]
        own_fade = jnp.exp2((own_top - top) * shade)
        near_fade = jnp.exp2((near_top - top) * shade)
        total = own_stats[1:2, both] * own_fade + near_stats[1:2, both] * near_fade
        for power in powers:
            total = total + jnp.sum(power, axis=0, keepdims=True)
        inverse = 1.0 / total
        sets = (
            (own_powers[:, both] * (own_fade * inverse), own_prob_grad[:, both], own_values_t),
            (near_powers[:, both] * (near_fade * inverse), near_prob_grad[:, both], near_values_t),
            (jnp.concatenate(powers, axis=0) * inverse, prob_grad, values_t),
        )
        rounded = [probs.astype(BF16) for probs, _, _ in sets]
        output_t = sum(dot(item[2][...], part, 1, 0) for item, part in zip(sets, rounded))
        output_t_ref[:, both] = output_t
        delta = jnp.sum(grad_t_ref[:, both].astype(F32) * output_t, axis=0, keepdims=True)
        targets = (
            (own_score_grad, own_key_acc, own_value_acc),
            (near_score_grad, near_key_acc, near_value_acc),
            (mate_score_grad, mate_key_acc, mate_value_acc),
        )
        for (probs, part_grad, _), part, (target, key_acc, value_acc) in zip(
            sets, rounded, targets
        ):
            score_grad = (probs * (part_grad - delta)).astype(BF16)
            target[:, both] = score_grad
            key_part = dot(score_grad, query, 1, 0)
            value_part = dot(part, grad, 1, 0)
            if pair == 0:
                key_acc[...] = key_part
                value_acc[...] = value_part
            else:
                key_acc[...] += key_part
                value_acc[...] += value_part

    for key_acc, value_acc, number, ref, start in (
        (mate_key_acc, mate_value_acc, 0, back_ref, 0),
        (mate_key_acc, mate_value_acc, 1, back_ref, rows),
        (own_key_acc, own_value_acc, 0, back_ref, 2 * rows),
        (near_key_acc, near_value_acc, 0, first_ref, 0),
        (near_key_acc, near_value_acc, 1, over_ref, 0),
        (own_key_acc, own_value_acc, 1, own_ref, 0),
    ):
        part = slice(number * rows, (number + 1) * rows)
        ref[start : start + rows, :dim] = (key_acc[part] * scaling).astype(ref.dtype)
        ref[start : start + rows, dim:] = value_acc[part].astype(ref.dtype)


def query_kernel(
    facts_ref,
    output_t_ref,
    own_score_grad,
    near_score_grad,
    mate_score_grad,
    own_keys_t,
    near_keys_t,
    mate_keys_t,
    attended_ref,
    query_grad_ref,
):
    rows = attended_ref.shape[0]
    dim = output_t_ref.shape[0]
    scaling = 1.0 / math.sqrt(dim)
    wide = 2 * rows
    valid = fact(facts_ref, VALID, wide)
    for pair in range(output_t_ref.shape[1] // wide):
        both = slice(pair * wide, (pair + 1) * wide)
        grad_t = (
            dot(own_keys_t[...], own_score_grad[:, both], 1, 0)
            + dot(near_keys_t[...], near_score_grad[:, both], 1, 0)
            + dot(mate_keys_t[...], mate_score_grad[:, both], 1, 0)
        )
        query_grad = (grad_t * scaling).T
        output = (output_t_ref[:, both] * valid).T
        for i in (0, 1):
            span = slice((2 * pair + i) * dim, (2 * pair + i + 1) * dim)
            part = slice(i * rows, (i + 1) * rows)
            attended_ref[:, span] = output[part].astype(BF16)
            query_grad_ref[:, span] = query_grad[part]


def merge_kernel(first_ref, over_ref, own_ref, back_ref, near_out, over_out, local_ref):
    rows = first_ref.shape[0]
    near_out[...] = (first_ref[...] + back_ref[:rows].astype(F32)).astype(BF16)
    over_out[...] = (over_ref[...] + back_ref[rows : 2 * rows].astype(F32)).astype(BF16)
    local_ref[...] = own_ref[...] + back_ref[2 * rows :].astype(F32)


def return_kernel(
    facts_ref, totals_ref, near_ref, local_ref, group_ref, seq_ref, cross_ref, out_ref, pay7, pay5
):
    rows = near_ref.shape[0]
    sums = [ref[...].astype(F32) for ref in (near_ref, group_ref, seq_ref, cross_ref)]
    out_ref[...] = local_ref[...] + (sums[0] + sums[2]) * fact(facts_ref, IS_PROMPT)
    for ref, base in ((pay7, FROM7), (pay5, FROM5)):
        total = sum(part * fact(facts_ref, base + i) for i, part in enumerate(sums))
        ref[:rows] = total.astype(BF16)
        store_tail(ref, rows, totals_ref[...])


def finish_kernel(
    facts_ref,
    local_ref,
    far7,
    far5,
    totals_ref,
    rest_ref,
    query_part_ref,
    query_grad_ref,
    key_grad_ref,
    value_grad_ref,
    loss_ref,
):
    rows, dim = key_grad_ref.shape
    totals = (totals_ref[...] + rest_ref[...]) + (decode(far7, rows) + decode(far5, rows))
    margin = totals - jnp.concatenate([totals[1:], totals[:1]], axis=0)
    slope = -BETA * margin
    small = jnp.exp(-jnp.abs(slope))
    bigger = 1.0 + small
    gap = bigger - 1.0
    log_part = jnp.where(
        gap == 0.0, small, jnp.log(bigger) * (small / jnp.where(gap == 0.0, 1.0, gap))
    )
    loss = jnp.maximum(slope, 0.0) + log_part
    weight = jnp.where(slope >= 0.0, 1.0, small) / bigger
    row = lax.broadcasted_iota(jnp.int32, (8, 128), 0)
    lane = lax.broadcasted_iota(jnp.int32, (8, 128), 1)
    in_lanes = jnp.sum(jnp.where(row == 2 * lane, loss, 0.0), axis=0, keepdims=True)
    loss_ref[...] = in_lanes[:, : loss_ref.shape[1]]
    mine = row.astype(F32) == fact(facts_ref, PAIR_ROW, 128)
    scale = jnp.sum(jnp.where(mine, weight, 0.0), axis=0, keepdims=True)
    far_sum = far7[:rows].astype(F32) + far5[:rows].astype(F32)
    total = local_ref[...] + far_sum * fact(facts_ref, IS_PROMPT)
    key_grad_ref[...] = (total[:, :dim] * scale).astype(BF16)
    value_grad_ref[...] = (total[:, dim:] * scale).astype(BF16)
    for start in range(0, query_grad_ref.shape[1], dim):
        span = slice(start, start + dim)
        query_grad_ref[:, span] = (query_part_ref[:, span] * scale).astype(BF16)


def call(kernel, out_shapes, operands, scratch=(), in_hbm=0, flops=0):
    single = not isinstance(out_shapes, (list, tuple))
    plain = len(operands) - in_hbm
    held = [
        pltpu.with_memory_space_constraint(operand, pltpu.HBM) for operand in operands[plain:]
    ]
    return pl.pallas_call(
        kernel,
        out_shape=out_shapes,
        in_specs=[VMEM_SPEC] * plain + [HBM_SPEC] * in_hbm,
        out_specs=VMEM_SPEC if single else [VMEM_SPEC] * len(out_shapes),
        scratch_shapes=list(scratch),
        compiler_params=pltpu.CompilerParams(vmem_limit_bytes=VMEM_BYTES),
        cost_estimate=pl.CostEstimate(flops=flops, bytes_accessed=0, transcendentals=0),
    )(*operands[:plain], *held)


def swap(count, turn):
    return [(i, i ^ turn) for i in range(count)]


def body(
    queries, key_heads, value_heads, cotangent, loss_mask, log_ratio, block_counts, response_order
):
    seq_count = lax.axis_size("seq")
    group_count = lax.axis_size("grp")
    head_count = lax.axis_size("head")
    rows = queries.shape[1]
    dim = key_heads.shape[2]
    width = queries.shape[2]
    heads = width // dim
    both = 2 * dim
    every = heads * rows
    shape = jax.ShapeDtypeStruct
    dma = pltpu.SemaphoreType.DMA
    tie = lax.optimization_barrier
    packed = shape((rows + TAIL, both), BF16)
    total_tile = shape((8, 128), F32)
    grads = shape((rows, both), BF16)
    grads_wide = shape((rows, both), F32)

    def along_grp(value, turn):
        return lax.ppermute(value, "grp", swap(group_count, turn))

    def along_seq(value, turn):
        return lax.ppermute(value, "seq", swap(seq_count, turn))

    def across(value):
        turns = [
            (s * group_count + g, (s ^ 2) * group_count + (g ^ 1))
            for s in range(seq_count)
            for g in range(group_count)
        ]
        return lax.ppermute(value, ("seq", "grp"), turns)

    def along_x(value, step):
        near = [(h, h ^ 2) for h in range(head_count)]
        round_way = [(h, (3 - h // 2) * 2 + h % 2) for h in range(head_count)]
        return lax.ppermute(value, "head", round_way if step else near)

    def along_y(value):
        turns = [
            (s * head_count + h, (s ^ 2) * head_count + (h ^ 1))
            for s in range(seq_count)
            for h in range(head_count)
        ]
        return lax.ppermute(value, ("seq", "head"), turns)

    own = call(
        pack_kernel, grads, (key_heads[0], value_heads[0]), scratch=[dma((2,))], in_hbm=2
    )
    far7 = along_grp(own, 7)
    far5 = along_grp(own, 5)
    own, response_order = tie((own, response_order))
    facts, totals, kept = call(
        facts_kernel,
        [shape((FACTS, both), F32), total_tile, shape((1, rows), F32)],
        (response_order, block_counts, loss_mask, log_ratio),
        scratch=[
            pltpu.SMEM(response_order.shape, jnp.int32),
            pltpu.SMEM(block_counts.shape, jnp.int32),
            pltpu.VMEM(loss_mask.shape, jnp.int32),
            pltpu.VMEM(log_ratio.shape, F32),
            dma((4,)),
        ],
        in_hbm=4,
    )
    mate_own = along_seq(own, 1)
    stacked = shape((every, dim), BF16)
    query_rows, grad_rows, grad_cols = call(
        prepare_kernel,
        [stacked, stacked, shape((dim, every), BF16)],
        (kept, queries[0], cotangent[0]),
        scratch=[pltpu.VMEM((every, dim), BF16), dma((2, heads))],
        in_hbm=2,
    )
    totals = totals + along_seq(totals, 1)
    part = along_x(totals, 0)
    far7, far5, totals, query_rows = tie((far7, far5, totals, query_rows))
    totals = totals + part
    to_group, to_seq, to_cross = call(
        route_kernel, [packed] * 3, (facts, totals, own, far7, far5)
    )
    from_seq = along_seq(to_seq, 2)
    from_group = along_grp(to_group, 1)
    from_cross = across(to_cross)

    def early(biases, is_own, left, right):
        return call(
            functools.partial(early_kernel, biases, is_own),
            [
                shape((2 * rows, every), F32),
                shape((2 * rows, every), F32),
                shape((8, every), F32),
                shape((dim, 2 * rows), BF16),
                shape((dim, 2 * rows), BF16),
            ],
            (facts, query_rows, grad_rows, left, right),
            scratch=[pltpu.VMEM((2 * rows, dim), BF16)] * 2,
            flops=8 * rows * every * dim,
        )

    own_set = early((BIAS_OWN, None), True, mate_own, own)
    from_cross, own_powers = tie((from_cross, own_set[0]))
    near, totals = call(
        select_kernel,
        [shape((2 * rows, both), BF16), total_tile],
        (facts, totals, own, far7, far5, from_group, from_seq, from_cross),
    )
    mate = along_seq(near, 1)
    near_set = early((BIAS_FIRST, BIAS_OVER), False, near, near)
    near_powers, totals = tie((near_set[0], totals))
    part = along_x(totals, 1)
    mate, near_powers = tie((mate, near_powers))
    back, first, over, local, output_t, own_sg, near_sg, mate_sg, mate_keys_t = call(
        late_kernel,
        [
            shape((3 * rows, both), BF16),
            grads_wide,
            grads_wide,
            grads_wide,
            shape((dim, every), F32),
            shape((2 * rows, every), BF16),
            shape((2 * rows, every), BF16),
            shape((2 * rows, every), BF16),
            shape((dim, 2 * rows), BF16),
        ],
        (
            facts,
            query_rows,
            grad_rows,
            grad_cols,
            own_powers,
            own_set[1],
            own_set[2],
            own_set[4],
            near_powers,
            near_set[1],
            near_set[2],
            near_set[4],
            mate,
        ),
        scratch=[
            pltpu.VMEM((2 * rows, dim), BF16),
            pltpu.VMEM((2 * rows, dim), BF16),
            pltpu.VMEM((dim, 2 * rows), BF16),
        ]
        + [pltpu.VMEM((2 * rows, dim), F32)] * 6,
        flops=40 * rows * every * dim,
    )
    back, totals = tie((back, totals))
    back, totals = tie((back, totals + part))
    part = along_y(totals)
    back = along_seq(back, 1)
    near_sum, over_sum, local = call(
        merge_kernel, [grads, grads, grads_wide], (first, over, local, back)
    )
    from_seq = along_seq(over_sum, 2)
    from_group = along_grp(near_sum, 1)
    from_cross = across(over_sum)
    totals = totals + part
    attended, query_part = call(
        query_kernel,
        [shape((rows, width), BF16), shape((rows, width), F32)],
        (facts, output_t, own_sg, near_sg, mate_sg, own_set[3], near_set[3], mate_keys_t),
        flops=12 * rows * every * dim,
    )
    from_cross, query_part = tie((from_cross, query_part))
    local, pay7, pay5 = call(
        return_kernel,
        [grads_wide, packed, packed],
        (facts, totals, near_sum, local, from_group, from_seq, from_cross),
    )
    far7 = along_grp(pay7, 7)
    far5 = along_grp(pay5, 5)
    rest = along_grp(totals, 2)
    query_grad, key_grad, value_grad, loss = call(
        finish_kernel,
        [
            shape((rows, width), BF16),
            shape((rows, dim), BF16),
            shape((rows, dim), BF16),
            shape((1, group_count // 2), F32),
        ],
        (facts, local, far7, far5, totals, rest, query_part),
    )
    return attended[None], query_grad[None], key_grad[None], value_grad[None], loss[0]


def solution(mesh):
    spec = P("grp", "seq", "head")
    in_specs = (spec, spec, spec, spec, P("grp", "seq"), P("grp", ("seq", "head")), P(), P())
    out_specs = (spec, spec, spec, spec, P())
    return jax.shard_map(body, mesh=mesh, in_specs=in_specs, out_specs=out_specs, check_vma=False)
```

```python
import functools
import math

import jax
import jax.numpy as jnp
from jax import lax
from jax.experimental import pallas as pl
from jax.experimental.pallas import tpu as pltpu
from jax.sharding import PartitionSpec as P

LEN_BLOCK = 128
BETA = 0.1
NEG_FILL = -1e30
LOG2_E = math.log2(math.e)
TAIL = 16
F32 = jnp.float32
BF16 = jnp.bfloat16
VMEM_BYTES = 40 * 1024 * 1024

VMEM_SPEC = pl.BlockSpec(memory_space=pltpu.VMEM)
HBM_SPEC = pl.BlockSpec(memory_space=pltpu.HBM)

FROM7, FROM5, IS_PROMPT, VALID, PAIR_ROW = 0, 4, 8, 9, 10
BIAS_FIRST, BIAS_MATE, BIAS_OVER, BIAS_CROSS, BIAS_OWN = 11, 12, 13, 14, 15
FACTS = 16


def dot(lhs, rhs, lhs_dim, rhs_dim):
    return lax.dot_general(
        lhs, rhs, (((lhs_dim,), (rhs_dim,)), ((), ())), preferred_element_type=F32
    )


def fact(facts_ref, row, width=None):
    return facts_ref[row : row + 1, :width]


def store_tail(ref, row, totals):
    high = totals.astype(BF16).astype(F32)
    rest = totals - high
    middle = rest.astype(BF16).astype(F32)
    low = rest - middle
    zero = jnp.zeros_like(middle)
    ref[row : row + TAIL, :128] = jnp.concatenate([high, low], axis=0).astype(BF16)
    ref[row : row + TAIL, 128:] = jnp.concatenate([middle, zero], axis=0).astype(BF16)


def decode(ref, row):
    left = ref[row : row + TAIL, :128].astype(F32)
    right = ref[row : row + TAIL, 128:].astype(F32)
    return (left[:8] + right[:8]) + left[8:]


def pack_kernel(key_ref, value_ref, out_ref, sems):
    dim = key_ref.shape[1]
    copies = [
        pltpu.make_async_copy(ref, out_ref.at[:, pl.ds(i * dim, dim)], sems.at[i])
        for i, ref in enumerate((key_ref, value_ref))
    ]
    for copy in copies:
        copy.start()
    for copy in copies:
        copy.wait()


def facts_kernel(
    order_hbm,
    counts_hbm,
    mask_hbm,
    ratio_hbm,
    facts_ref,
    totals_ref,
    kept_ref,
    order_ref,
    counts_ref,
    mask_ref,
    ratio_ref,
    sems,
):
    copies = [
        pltpu.make_async_copy(source, target, sems.at[i])
        for i, (source, target) in enumerate(
            (
                (order_hbm, order_ref),
                (counts_hbm, counts_ref),
                (mask_hbm, mask_ref),
                (ratio_hbm, ratio_ref),
            )
        )
    ]
    for copy in copies:
        copy.start()
    seq = lax.axis_index("seq")
    grp = lax.axis_index("grp")
    head = lax.axis_index("head")
    pairs = lax.axis_size("grp") // 2
    is_response = grp >= pairs
    for copy in copies:
        copy.wait()

    def pair_of(group, half):
        return order_ref[jnp.where(is_response, 2 * (group - pairs), 0) + half] // 2

    def put(row, value):
        facts_ref[row : row + 1, :] = jnp.full((1, facts_ref.shape[1]), value, F32)

    def flag(row, condition, yes=1.0, no=0.0):
        put(row, jnp.where(condition, yes, no).astype(F32))

    half = seq // 2
    slots = [pair_of(group, side) for side in (half, 1 - half) for group in (grp, grp ^ 1)]
    for number, pair in enumerate(slots):
        flag(FROM7 + number, jnp.logical_and(is_response, pair == (grp ^ 7)))
        flag(FROM5 + number, jnp.logical_and(is_response, pair == (grp ^ 5)))
    slot = jnp.where(is_response, 2 * (grp - pairs), 0) + half
    filled = seq % 2 < counts_ref[slot]
    valid = jnp.logical_or(jnp.logical_not(is_response), filled)
    my_pair = jnp.where(is_response, order_ref[slot] // 2, jnp.minimum(grp, pairs - 1))
    flag(IS_PROMPT, jnp.logical_not(is_response))
    flag(VALID, valid)
    put(PAIR_ROW, (2 * my_pair).astype(F32))
    flag(BIAS_FIRST, is_response, 0.0, NEG_FILL)
    flag(BIAS_MATE, jnp.logical_or(is_response, seq % 2 == 1), 0.0, NEG_FILL)
    flag(BIAS_OVER, jnp.logical_or(is_response, seq >= 2), 0.0, NEG_FILL)
    flag(BIAS_CROSS, jnp.logical_or(is_response, seq >= 2), 0.0, NEG_FILL)
    flag(BIAS_OWN, jnp.logical_and(is_response, seq % 2 == 1), 0.0, NEG_FILL)

    piece = ratio_ref.shape[1]
    lane = lax.broadcasted_iota(jnp.int32, (piece, 128), 1)
    spot = lax.broadcasted_iota(jnp.int32, (piece, 128), 0)
    place_at = (lane == spot + head * piece).astype(F32)
    spread = lax.dot_general(
        jnp.broadcast_to(ratio_ref[...], (8, piece)),
        place_at,
        (((1,), (0,)), ((), ())),
        precision=lax.Precision.HIGHEST,
        preferred_element_type=F32,
    )
    kept = mask_ref[...] > 0
    partial = jnp.sum(jnp.where(kept, spread[:1], 0.0), axis=1, keepdims=True)
    row = lax.broadcasted_iota(jnp.int32, (8, 128), 0)
    mine = jnp.where(jnp.logical_and(is_response, filled), order_ref[slot], -1)
    totals_ref[...] = jnp.where(row == mine, jnp.broadcast_to(partial, (8, 128)), 0.0)
    negative = jnp.logical_and(is_response, order_ref[slot] % 2 == 0)
    sign = jnp.where(valid, jnp.where(negative, -1.0, 1.0), 0.0).astype(F32)
    kept_ref[...] = jnp.where(kept, sign, 0.0)


def prepare_kernel(kept_ref, query_hbm, cot_hbm, query_ref, grad_ref, grad_t_ref, cots, sems):
    rows = kept_ref.shape[1]
    dim = query_ref.shape[1]
    heads = query_ref.shape[0] // rows
    copies = []
    for i in range(heads):
        for j, (source, target) in enumerate(((cot_hbm, cots), (query_hbm, query_ref))):
            copies.append(
                pltpu.make_async_copy(
                    source.at[:, pl.ds(i * dim, dim)],
                    target.at[pl.ds(i * rows, rows)],
                    sems.at[j, i],
                )
            )
    for copy in copies:
        copy.start()
    kept_rows = jnp.broadcast_to(kept_ref[...], (rows, rows)).T
    for copy in copies:
        copy.wait()
    for i in range(heads):
        part = slice(i * rows, (i + 1) * rows)
        grad = (cots[part].astype(F32) * kept_rows).astype(BF16)
        grad_ref[part] = grad
        grad_t_ref[:, part] = grad.T


def route_kernel(facts_ref, own_ref, far7, far5, group_ref, seq_ref, cross_ref):
    for number, ref in ((1, group_ref), (2, seq_ref), (3, cross_ref)):
        picked = far7[...].astype(F32) * fact(facts_ref, FROM7 + number)
        picked = picked + far5[...].astype(F32) * fact(facts_ref, FROM5 + number)
        if number == 2:
            picked = picked + own_ref[...].astype(F32) * fact(facts_ref, IS_PROMPT)
        ref[...] = picked.astype(BF16)


def select_kernel(facts_ref, own_ref, far7, far5, group_ref, seq_ref, cross_ref, near_ref):
    rows = own_ref.shape[0]
    first = far7[...].astype(F32) * fact(facts_ref, FROM7)
    first = first + far5[...].astype(F32) * fact(facts_ref, FROM5)
    first = first + own_ref[...].astype(F32) * fact(facts_ref, IS_PROMPT)
    near_ref[:rows] = (first + group_ref[...].astype(F32)).astype(BF16)
    near_ref[rows:] = (seq_ref[...].astype(F32) + cross_ref[...].astype(F32)).astype(BF16)


def load_blocks(blocks, keys, values, keys_t, values_t):
    dim = keys.shape[1]
    rows = keys.shape[0] // len(blocks)
    for number, (ref, start) in enumerate(blocks):
        part = slice(number * rows, (number + 1) * rows)
        key_part = ref[start : start + rows, :dim]
        value_part = ref[start : start + rows, dim:]
        keys[part] = key_part
        values[part] = value_part
        keys_t[:, part] = key_part.T
        values_t[:, part] = value_part.T


def early_kernel(
    biases,
    is_own,
    facts_ref,
    query_ref,
    grad_ref,
    left_ref,
    right_ref,
    powers_ref,
    prob_grad_ref,
    stats_ref,
    keys_t,
    values_t,
    keys,
    values,
):
    rows = keys.shape[0] // 2
    heads = query_ref.shape[0] // rows
    shade = LOG2_E / math.sqrt(keys.shape[1])
    start = 0 if is_own else rows
    load_blocks(((left_ref, 0), (right_ref, start)), keys, values, keys_t, values_t)
    wide = 2 * rows
    key_id = lax.broadcasted_iota(jnp.int32, (rows, wide), 0)
    row_id = lax.broadcasted_iota(jnp.int32, (rows, wide), 1) % rows
    causal = key_id <= row_id
    bias = [fact(facts_ref, row, wide) if row is not None else 0.0 for row in biases]
    for pair in range(heads // 2):
        both = slice(pair * wide, (pair + 1) * wide)
        scores = dot(keys[...], query_ref[both], 1, 1)
        prob_grad_ref[:, both] = dot(values[...], grad_ref[both], 1, 1)
        pieces = [scores[:rows], scores[rows:]]
        if is_own:
            pieces[1] = jnp.where(causal, pieces[1], NEG_FILL)
        tops = [jnp.max(piece, axis=0, keepdims=True) for piece in pieces]
        top = jnp.maximum(tops[0] + bias[0], tops[1] + bias[1])
        total = jnp.zeros_like(top)
        for i, piece in enumerate(pieces):
            power = jnp.exp2(piece * shade + (bias[i] - shade * top))
            total = total + jnp.sum(power, axis=0, keepdims=True)
            powers_ref[i * rows : (i + 1) * rows, both] = power
        stats_ref[0:1, both] = top
        stats_ref[1:2, both] = total


def late_kernel(
    facts_ref,
    query_ref,
    grad_ref,
    grad_t_ref,
    own_powers,
    own_prob_grad,
    own_stats,
    own_values_t,
    near_powers,
    near_prob_grad,
    near_stats,
    near_values_t,
    mate_ref,
    back_ref,
    first_ref,
    over_ref,
    output_t_ref,
    own_rounded,
    own_score_grad,
    near_score_grad,
    mate_score_grad,
    keys_t,
    keys,
    values,
    values_t,
    powers,
    prob_grad,
    stats,
    factors,
    near_rounded,
    mate_rounded,
):
    rows, dim = keys.shape[0] // 2, keys.shape[1]
    heads = query_ref.shape[0] // rows
    scaling = 1.0 / math.sqrt(dim)
    shade = LOG2_E * scaling
    load_blocks(((mate_ref, 0), (mate_ref, rows)), keys, values, keys_t, values_t)
    wide = 2 * rows
    spans = [slice(pair * wide, (pair + 1) * wide) for pair in range(heads // 2)]
    bias = [fact(facts_ref, row, wide) for row in (BIAS_MATE, BIAS_CROSS)]
    for both in spans:
        scores = dot(keys[...], query_ref[both], 1, 1)
        prob_grad[:, both] = dot(values[...], grad_ref[both], 1, 1)
        pieces = [scores[:rows], scores[rows:]]
        tops = [jnp.max(pieces[i], axis=0, keepdims=True) + bias[i] for i in (0, 1)]
        top = jnp.maximum(tops[0], tops[1])
        total = jnp.zeros_like(top)
        for i, piece in enumerate(pieces):
            power = jnp.exp2(piece * shade + (bias[i] - shade * top))
            total = total + jnp.sum(power, axis=0, keepdims=True)
            powers[i * rows : (i + 1) * rows, both] = power
        stats[0:1, both] = top
        stats[1:2, both] = total

    sets = (
        (own_powers, own_prob_grad, own_stats, own_values_t, own_rounded, own_score_grad),
        (near_powers, near_prob_grad, near_stats, near_values_t, near_rounded, near_score_grad),
        (powers, prob_grad, stats, values_t, mate_rounded, mate_score_grad),
    )
    for both in spans:
        tops = [item[2][0:1, both] for item in sets]
        top = jnp.maximum(jnp.maximum(tops[0], tops[1]), tops[2])
        fades = [jnp.exp2((part - top) * shade) for part in tops]
        total = sum(item[2][1:2, both] * fade for item, fade in zip(sets, fades))
        inverse = 1.0 / total
        output_t = None
        for i, item in enumerate(sets):
            factor = fades[i] * inverse
            factors[i : i + 1, both] = factor
            rounded = (item[0][:, both] * factor).astype(BF16)
            item[4][:, both] = rounded
            part = dot(item[3][...], rounded, 1, 0)
            output_t = part if output_t is None else output_t + part
        output_t_ref[:, both] = output_t
        factors[3:4, both] = jnp.sum(
            grad_t_ref[:, both].astype(F32) * output_t, axis=0, keepdims=True
        )

    for both in spans:
        delta = factors[3:4, both]
        for i, item in enumerate(sets):
            probs = item[0][:, both] * factors[i : i + 1, both]
            item[5][:, both] = (probs * (item[1][:, both] - delta)).astype(BF16)

    for item, near_out, over_out in (
        (sets[2], (back_ref, 0), (back_ref, rows)),
        (sets[1], (first_ref, 0), (over_ref, 0)),
    ):
        key_part = dot(item[5][...], query_ref[...], 1, 0) * scaling
        value_part = dot(item[4][...], grad_ref[...], 1, 0)
        for number, (ref, start) in enumerate((near_out, over_out)):
            part = slice(number * rows, (number + 1) * rows)
            ref[start : start + rows, :dim] = key_part[part].astype(ref.dtype)
            ref[start : start + rows, dim:] = value_part[part].astype(ref.dtype)


def query_kernel(
    facts_ref,
    output_t_ref,
    own_score_grad,
    near_score_grad,
    mate_score_grad,
    own_keys_t,
    near_keys_t,
    mate_keys_t,
    own_rounded,
    query_ref,
    grad_ref,
    attended_ref,
    query_grad_ref,
    back_ref,
    local_ref,
    key_acc,
    value_acc,
):
    rows = attended_ref.shape[0]
    dim = output_t_ref.shape[0]
    scaling = 1.0 / math.sqrt(dim)
    wide = 2 * rows
    valid = fact(facts_ref, VALID, wide)
    for pair in range(output_t_ref.shape[1] // wide):
        both = slice(pair * wide, (pair + 1) * wide)
        grad_t = (
            dot(own_keys_t[...], own_score_grad[:, both], 1, 0)
            + dot(near_keys_t[...], near_score_grad[:, both], 1, 0)
            + dot(mate_keys_t[...], mate_score_grad[:, both], 1, 0)
        )
        key_part = dot(own_score_grad[:, both], query_ref[both], 1, 0)
        value_part = dot(own_rounded[:, both], grad_ref[both], 1, 0)
        if pair == 0:
            key_acc[...] = key_part
            value_acc[...] = value_part
        else:
            key_acc[...] += key_part
            value_acc[...] += value_part
        query_grad = (grad_t * scaling).T
        output = (output_t_ref[:, both] * valid).T
        for i in (0, 1):
            span = slice((2 * pair + i) * dim, (2 * pair + i + 1) * dim)
            part = slice(i * rows, (i + 1) * rows)
            attended_ref[:, span] = output[part].astype(BF16)
            query_grad_ref[:, span] = query_grad[part]
    for number, ref in ((0, back_ref), (1, local_ref)):
        part = slice(number * rows, (number + 1) * rows)
        ref[:, :dim] = (key_acc[part] * scaling).astype(ref.dtype)
        ref[:, dim:] = value_acc[part].astype(ref.dtype)


def merge_kernel(totals_ref, first_ref, over_ref, back_ref, near_out, over_out):
    rows = first_ref.shape[0]
    near_out[:rows] = (first_ref[...] + back_ref[:rows].astype(F32)).astype(BF16)
    over_out[:rows] = (over_ref[...] + back_ref[rows:].astype(F32)).astype(BF16)
    store_tail(near_out, rows, totals_ref[...])
    store_tail(over_out, rows, totals_ref[...])


def return_kernel(
    facts_ref,
    totals_ref,
    near_ref,
    group_ref,
    seq_ref,
    cross_ref,
    prompt_ref,
    pay7,
    pay5,
    sum_ref,
):
    rows = prompt_ref.shape[0]
    refs = (near_ref, group_ref, seq_ref, cross_ref)
    sums = [ref[:rows].astype(F32) for ref in refs]
    prompt_ref[...] = (sums[0] + sums[2]) * fact(facts_ref, IS_PROMPT)
    totals = (totals_ref[...] + decode(group_ref, rows)) + (
        decode(seq_ref, rows) + decode(cross_ref, rows)
    )
    sum_ref[...] = totals
    for ref, base in ((pay7, FROM7), (pay5, FROM5)):
        total = sum(part * fact(facts_ref, base + i) for i, part in enumerate(sums))
        ref[:rows] = total.astype(BF16)
        store_tail(ref, rows, totals)


def finish_kernel(
    facts_ref,
    local_ref,
    mate_ref,
    prompt_ref,
    far7,
    far5,
    totals_ref,
    rest_ref,
    query_part_ref,
    query_grad_ref,
    key_grad_ref,
    value_grad_ref,
    loss_ref,
):
    rows, dim = key_grad_ref.shape
    totals = (totals_ref[...] + rest_ref[...]) + (decode(far7, rows) + decode(far5, rows))
    margin = totals - jnp.concatenate([totals[1:], totals[:1]], axis=0)
    slope = -BETA * margin
    small = jnp.exp(-jnp.abs(slope))
    bigger = 1.0 + small
    gap = bigger - 1.0
    log_part = jnp.where(
        gap == 0.0, small, jnp.log(bigger) * (small / jnp.where(gap == 0.0, 1.0, gap))
    )
    loss = jnp.maximum(slope, 0.0) + log_part
    weight = jnp.where(slope >= 0.0, 1.0, small) / bigger
    row = lax.broadcasted_iota(jnp.int32, (8, 128), 0)
    lane = lax.broadcasted_iota(jnp.int32, (8, 128), 1)
    in_lanes = jnp.sum(jnp.where(row == 2 * lane, loss, 0.0), axis=0, keepdims=True)
    loss_ref[...] = in_lanes[:, : loss_ref.shape[1]]
    mine = row.astype(F32) == fact(facts_ref, PAIR_ROW, 128)
    scale = jnp.sum(jnp.where(mine, weight, 0.0), axis=0, keepdims=True)
    far_sum = far7[:rows].astype(F32) + far5[:rows].astype(F32)
    total = local_ref[...] + mate_ref[...].astype(F32) + prompt_ref[...]
    total = total + far_sum * fact(facts_ref, IS_PROMPT)
    key_grad_ref[...] = (total[:, :dim] * scale).astype(BF16)
    value_grad_ref[...] = (total[:, dim:] * scale).astype(BF16)
    for start in range(0, query_grad_ref.shape[1], dim):
        span = slice(start, start + dim)
        query_grad_ref[:, span] = (query_part_ref[:, span] * scale).astype(BF16)


def call(kernel, out_shapes, operands, scratch=(), in_hbm=0, flops=0):
    single = not isinstance(out_shapes, (list, tuple))
    plain = len(operands) - in_hbm
    held = [
        pltpu.with_memory_space_constraint(operand, pltpu.HBM) for operand in operands[plain:]
    ]
    return pl.pallas_call(
        kernel,
        out_shape=out_shapes,
        in_specs=[VMEM_SPEC] * plain + [HBM_SPEC] * in_hbm,
        out_specs=VMEM_SPEC if single else [VMEM_SPEC] * len(out_shapes),
        scratch_shapes=list(scratch),
        compiler_params=pltpu.CompilerParams(vmem_limit_bytes=VMEM_BYTES),
        cost_estimate=pl.CostEstimate(flops=flops, bytes_accessed=0, transcendentals=0),
    )(*operands[:plain], *held)


def swap(count, turn):
    return [(i, i ^ turn) for i in range(count)]


def body(
    queries, key_heads, value_heads, cotangent, loss_mask, log_ratio, block_counts, response_order
):
    seq_count = lax.axis_size("seq")
    group_count = lax.axis_size("grp")
    head_count = lax.axis_size("head")
    rows = queries.shape[1]
    dim = key_heads.shape[2]
    width = queries.shape[2]
    heads = width // dim
    both = 2 * dim
    every = heads * rows
    shape = jax.ShapeDtypeStruct
    dma = pltpu.SemaphoreType.DMA
    tie = lax.optimization_barrier
    packed = shape((rows + TAIL, both), BF16)
    total_tile = shape((8, 128), F32)
    grads = shape((rows, both), BF16)
    grads_wide = shape((rows, both), F32)

    def along_grp(value, turn):
        return lax.ppermute(value, "grp", swap(group_count, turn))

    def along_seq(value, turn):
        return lax.ppermute(value, "seq", swap(seq_count, turn))

    def across(value):
        turns = [
            (s * group_count + g, (s ^ 2) * group_count + (g ^ 1))
            for s in range(seq_count)
            for g in range(group_count)
        ]
        return lax.ppermute(value, ("seq", "grp"), turns)

    def along_x(value, step):
        near = [(h, h ^ 2) for h in range(head_count)]
        round_way = [(h, (3 - h // 2) * 2 + h % 2) for h in range(head_count)]
        return lax.ppermute(value, "head", round_way if step else near)

    def along_y(value):
        return lax.ppermute(value, "head", swap(head_count, 1))

    own = call(
        pack_kernel, grads, (key_heads[0], value_heads[0]), scratch=[dma((2,))], in_hbm=2
    )
    far7 = along_grp(own, 7)
    far5 = along_grp(own, 5)
    own, response_order = tie((own, response_order))
    facts, totals, kept = call(
        facts_kernel,
        [shape((FACTS, both), F32), total_tile, shape((1, rows), F32)],
        (response_order, block_counts, loss_mask, log_ratio),
        scratch=[
            pltpu.SMEM(response_order.shape, jnp.int32),
            pltpu.SMEM(block_counts.shape, jnp.int32),
            pltpu.VMEM(loss_mask.shape, jnp.int32),
            pltpu.VMEM(log_ratio.shape, F32),
            dma((4,)),
        ],
        in_hbm=4,
    )
    mate_own = along_seq(own, 1)
    stacked = shape((every, dim), BF16)
    query_rows, grad_rows, grad_cols = call(
        prepare_kernel,
        [stacked, stacked, shape((dim, every), BF16)],
        (kept, queries[0], cotangent[0]),
        scratch=[pltpu.VMEM((every, dim), BF16), dma((2, heads))],
        in_hbm=2,
    )
    part = along_y(totals)
    far7, far5, totals, query_rows = tie((far7, far5, totals, query_rows))
    totals = totals + part
    far7, far5, totals = tie((far7, far5, totals))
    to_group, to_seq, to_cross = call(route_kernel, [grads] * 3, (facts, own, far7, far5))
    from_seq = along_seq(to_seq, 2)
    from_group = along_grp(to_group, 1)
    from_cross = across(to_cross)

    def early(biases, is_own, left, right):
        return call(
            functools.partial(early_kernel, biases, is_own),
            [
                shape((2 * rows, every), F32),
                shape((2 * rows, every), F32),
                shape((8, every), F32),
                shape((dim, 2 * rows), BF16),
                shape((dim, 2 * rows), BF16),
            ],
            (facts, query_rows, grad_rows, left, right),
            scratch=[pltpu.VMEM((2 * rows, dim), BF16)] * 2,
            flops=8 * rows * every * dim,
        )

    own_set = early((BIAS_OWN, None), True, mate_own, own)
    totals = totals + along_x(totals, 1)
    from_cross, own_powers, totals = tie((from_cross, own_set[0], totals))
    near = call(
        select_kernel,
        shape((2 * rows, both), BF16),
        (facts, own, far7, far5, from_group, from_seq, from_cross),
    )
    mate = along_seq(near, 1)
    near_set = early((BIAS_FIRST, BIAS_OVER), False, near, near)
    near_powers, totals = tie((near_set[0], totals))
    part = along_x(totals, 0)
    mate, near_powers = tie((mate, near_powers))
    back, first, over, output_t, own_rounded, own_sg, near_sg, mate_sg, mate_keys_t = call(
        late_kernel,
        [
            shape((2 * rows, both), BF16),
            grads_wide,
            grads_wide,
            shape((dim, every), F32),
            shape((2 * rows, every), BF16),
            shape((2 * rows, every), BF16),
            shape((2 * rows, every), BF16),
            shape((2 * rows, every), BF16),
            shape((dim, 2 * rows), BF16),
        ],
        (
            facts,
            query_rows,
            grad_rows,
            grad_cols,
            own_powers,
            own_set[1],
            own_set[2],
            own_set[4],
            near_powers,
            near_set[1],
            near_set[2],
            near_set[4],
            mate,
        ),
        scratch=[
            pltpu.VMEM((2 * rows, dim), BF16),
            pltpu.VMEM((2 * rows, dim), BF16),
            pltpu.VMEM((dim, 2 * rows), BF16),
        ]
        + [pltpu.VMEM((2 * rows, every), F32)] * 2
        + [pltpu.VMEM((8, every), F32)] * 2
        + [pltpu.VMEM((2 * rows, every), BF16)] * 2,
        flops=40 * rows * every * dim,
    )
    back, totals = tie((back, totals))
    back, totals = tie((back, totals + part))
    back = along_seq(back, 1)
    totals = totals + along_seq(totals, 1)
    near_sum, over_sum = call(merge_kernel, [packed, packed], (totals, first, over, back))
    from_seq = along_seq(over_sum, 2)
    from_group = along_grp(near_sum, 1)
    from_cross = across(over_sum)
    attended, query_part, own_back, local = call(
        query_kernel,
        [shape((rows, width), BF16), shape((rows, width), F32), grads, grads_wide],
        (
            facts,
            output_t,
            own_sg,
            near_sg,
            mate_sg,
            own_set[3],
            near_set[3],
            mate_keys_t,
            own_rounded,
            query_rows,
            grad_rows,
        ),
        scratch=[pltpu.VMEM((2 * rows, dim), F32)] * 2,
        flops=20 * rows * every * dim,
    )
    from_cross, query_part = tie((from_cross, query_part))
    from_prompt, pay7, pay5, totals = call(
        return_kernel,
        [grads_wide, packed, packed, total_tile],
        (facts, totals, near_sum, from_group, from_seq, from_cross),
    )
    far7 = along_grp(pay7, 7)
    far5 = along_grp(pay5, 5)
    own_back = along_seq(own_back, 1)
    rest = along_grp(totals, 2)
    query_grad, key_grad, value_grad, loss = call(
        finish_kernel,
        [
            shape((rows, width), BF16),
            shape((rows, dim), BF16),
            shape((rows, dim), BF16),
            shape((1, group_count // 2), F32),
        ],
        (facts, local, own_back, from_prompt, far7, far5, totals, rest, query_part),
    )
    return attended[None], query_grad[None], key_grad[None], value_grad[None], loss[0]


def solution(mesh):
    spec = P("grp", "seq", "head")
    in_specs = (spec, spec, spec, spec, P("grp", "seq"), P("grp", ("seq", "head")), P(), P())
    out_specs = (spec, spec, spec, spec, P())
    return jax.shard_map(body, mesh=mesh, in_specs=in_specs, out_specs=out_specs, check_vma=False)
```

```python
import functools
import math

import jax
import jax.numpy as jnp
from jax import lax
from jax.experimental import pallas as pl
from jax.experimental.pallas import tpu as pltpu
from jax.sharding import PartitionSpec as P

LEN_BLOCK = 128
BETA = 0.1
NEG_FILL = -1e30
LOG2_E = math.log2(math.e)
TAIL = 16
F32 = jnp.float32
BF16 = jnp.bfloat16
VMEM_BYTES = 40 * 1024 * 1024

VMEM_SPEC = pl.BlockSpec(memory_space=pltpu.VMEM)
HBM_SPEC = pl.BlockSpec(memory_space=pltpu.HBM)

FROM6, FROM5, IS_PROMPT, VALID, PAIR_ROW = 0, 4, 8, 9, 10
BIAS_FIRST, BIAS_MATE, BIAS_OVER, BIAS_CROSS, BIAS_OWN = 11, 12, 13, 14, 15
FACTS = 16


def dot(lhs, rhs, lhs_dim, rhs_dim):
    return lax.dot_general(
        lhs, rhs, (((lhs_dim,), (rhs_dim,)), ((), ())), preferred_element_type=F32
    )


def fact(facts_ref, row, width=None):
    return facts_ref[row : row + 1, :width]


def store_tail(ref, row, totals):
    high = totals.astype(BF16).astype(F32)
    rest = totals - high
    middle = rest.astype(BF16).astype(F32)
    low = rest - middle
    zero = jnp.zeros_like(middle)
    ref[row : row + TAIL, :128] = jnp.concatenate([high, low], axis=0).astype(BF16)
    ref[row : row + TAIL, 128:] = jnp.concatenate([middle, zero], axis=0).astype(BF16)


def decode(ref, row):
    left = ref[row : row + TAIL, :128].astype(F32)
    right = ref[row : row + TAIL, 128:].astype(F32)
    return (left[:8] + right[:8]) + left[8:]


def pack_kernel(key_ref, value_ref, out_ref, sems):
    dim = key_ref.shape[1]
    copies = [
        pltpu.make_async_copy(ref, out_ref.at[:, pl.ds(i * dim, dim)], sems.at[i])
        for i, ref in enumerate((key_ref, value_ref))
    ]
    for copy in copies:
        copy.start()
    for copy in copies:
        copy.wait()


def facts_kernel(
    order_hbm,
    counts_hbm,
    mask_hbm,
    ratio_hbm,
    facts_ref,
    totals_ref,
    kept_ref,
    order_ref,
    counts_ref,
    mask_ref,
    ratio_ref,
    sems,
):
    copies = [
        pltpu.make_async_copy(source, target, sems.at[i])
        for i, (source, target) in enumerate(
            (
                (order_hbm, order_ref),
                (counts_hbm, counts_ref),
                (mask_hbm, mask_ref),
                (ratio_hbm, ratio_ref),
            )
        )
    ]
    for copy in copies:
        copy.start()
    seq = lax.axis_index("seq")
    grp = lax.axis_index("grp")
    head = lax.axis_index("head")
    pairs = lax.axis_size("grp") // 2
    is_response = grp >= pairs
    for copy in copies:
        copy.wait()

    def pair_of(group, half):
        return order_ref[jnp.where(is_response, 2 * (group - pairs), 0) + half] // 2

    def put(row, value):
        facts_ref[row : row + 1, :] = jnp.full((1, facts_ref.shape[1]), value, F32)

    def flag(row, condition, yes=1.0, no=0.0):
        put(row, jnp.where(condition, yes, no).astype(F32))

    half = seq // 2
    slots = [pair_of(group, side) for side in (half, 1 - half) for group in (grp, grp ^ 1)]
    for number, pair in enumerate(slots):
        flag(FROM6 + number, jnp.logical_and(is_response, pair == (grp ^ 6)))
        flag(FROM5 + number, jnp.logical_and(is_response, pair == (grp ^ 5)))
    slot = jnp.where(is_response, 2 * (grp - pairs), 0) + half
    filled = seq % 2 < counts_ref[slot]
    valid = jnp.logical_or(jnp.logical_not(is_response), filled)
    my_pair = jnp.where(is_response, order_ref[slot] // 2, jnp.minimum(grp, pairs - 1))
    flag(IS_PROMPT, jnp.logical_not(is_response))
    flag(VALID, valid)
    put(PAIR_ROW, (2 * my_pair).astype(F32))
    flag(BIAS_FIRST, is_response, 0.0, NEG_FILL)
    flag(BIAS_MATE, jnp.logical_or(is_response, seq % 2 == 1), 0.0, NEG_FILL)
    flag(BIAS_OVER, jnp.logical_or(is_response, seq >= 2), 0.0, NEG_FILL)
    flag(BIAS_CROSS, jnp.logical_or(is_response, seq >= 2), 0.0, NEG_FILL)
    flag(BIAS_OWN, jnp.logical_and(is_response, seq % 2 == 1), 0.0, NEG_FILL)

    piece = ratio_ref.shape[1]
    lane = lax.broadcasted_iota(jnp.int32, (piece, 128), 1)
    spot = lax.broadcasted_iota(jnp.int32, (piece, 128), 0)
    place_at = (lane == spot + head * piece).astype(F32)
    spread = lax.dot_general(
        jnp.broadcast_to(ratio_ref[...], (8, piece)),
        place_at,
        (((1,), (0,)), ((), ())),
        precision=lax.Precision.HIGHEST,
        preferred_element_type=F32,
    )
    kept = mask_ref[...] > 0
    partial = jnp.sum(jnp.where(kept, spread[:1], 0.0), axis=1, keepdims=True)
    row = lax.broadcasted_iota(jnp.int32, (8, 128), 0)
    mine = jnp.where(jnp.logical_and(is_response, filled), order_ref[slot], -1)
    totals_ref[...] = jnp.where(row == mine, jnp.broadcast_to(partial, (8, 128)), 0.0)
    negative = jnp.logical_and(is_response, order_ref[slot] % 2 == 0)
    sign = jnp.where(valid, jnp.where(negative, -1.0, 1.0), 0.0).astype(F32)
    kept_ref[...] = jnp.where(kept, sign, 0.0)


def prepare_kernel(
    kept_ref, query_hbm, cot_hbm, query_ref, query_t_ref, grad_ref, grad_t_ref, cots, sems
):
    rows = kept_ref.shape[1]
    dim = query_ref.shape[1]
    heads = query_ref.shape[0] // rows
    copies = []
    for i in range(heads):
        for j, (source, target) in enumerate(((cot_hbm, cots), (query_hbm, query_ref))):
            copies.append(
                pltpu.make_async_copy(
                    source.at[:, pl.ds(i * dim, dim)],
                    target.at[pl.ds(i * rows, rows)],
                    sems.at[j, i],
                )
            )
    for copy in copies:
        copy.start()
    kept_rows = jnp.broadcast_to(kept_ref[...], (rows, rows)).T
    for copy in copies:
        copy.wait()
    for i in range(heads):
        part = slice(i * rows, (i + 1) * rows)
        grad = (cots[part].astype(F32) * kept_rows).astype(BF16)
        grad_ref[part] = grad
        grad_t_ref[:, part] = grad.T
        query_t_ref[:, part] = query_ref[part].T


def route_kernel(facts_ref, totals_ref, own_ref, far6, far5, group_ref, seq_ref, cross_ref):
    rows = own_ref.shape[0]
    for number, ref in ((1, group_ref), (2, seq_ref), (3, cross_ref)):
        picked = far6[...].astype(F32) * fact(facts_ref, FROM6 + number)
        picked = picked + far5[...].astype(F32) * fact(facts_ref, FROM5 + number)
        if number == 2:
            picked = picked + own_ref[...].astype(F32) * fact(facts_ref, IS_PROMPT)
        ref[:rows] = picked.astype(BF16)
        store_tail(ref, rows, totals_ref[...])


def select_kernel(
    facts_ref, totals_ref, own_ref, far6, far5, group_ref, seq_ref, cross_ref, near_ref, sum_ref
):
    rows = own_ref.shape[0]
    first = far6[...].astype(F32) * fact(facts_ref, FROM6)
    first = first + far5[...].astype(F32) * fact(facts_ref, FROM5)
    first = first + own_ref[...].astype(F32) * fact(facts_ref, IS_PROMPT)
    near_ref[:rows] = (first + group_ref[:rows].astype(F32)).astype(BF16)
    near_ref[rows:] = (seq_ref[:rows].astype(F32) + cross_ref[:rows].astype(F32)).astype(BF16)
    totals = (totals_ref[...] + decode(group_ref, rows)) + (
        decode(seq_ref, rows) + decode(cross_ref, rows)
    )
    sum_ref[...] = jnp.concatenate([totals] * (sum_ref.shape[0] // 8), axis=0)


def load_blocks(blocks, keys, values, keys_t, values_t):
    dim = keys.shape[1]
    rows = keys.shape[0] // len(blocks)
    for number, (ref, start) in enumerate(blocks):
        part = slice(number * rows, (number + 1) * rows)
        key_part = ref[start : start + rows, :dim]
        value_part = ref[start : start + rows, dim:]
        keys[part] = key_part
        values[part] = value_part
        keys_t[:, part] = key_part.T
        values_t[:, part] = value_part.T


def early_kernel(
    biases,
    is_own,
    facts_ref,
    query_ref,
    grad_ref,
    left_ref,
    right_ref,
    powers_ref,
    prob_grad_ref,
    stats_ref,
    keys_t,
    values_t,
    keys,
    values,
):
    rows = keys.shape[0] // 2
    heads = query_ref.shape[0] // rows
    shade = LOG2_E / math.sqrt(keys.shape[1])
    start = 0 if is_own else rows
    load_blocks(((left_ref, 0), (right_ref, start)), keys, values, keys_t, values_t)
    wide = 2 * rows
    key_id = lax.broadcasted_iota(jnp.int32, (rows, wide), 0)
    row_id = lax.broadcasted_iota(jnp.int32, (rows, wide), 1) % rows
    causal = key_id <= row_id
    bias = [fact(facts_ref, row, wide) if row is not None else 0.0 for row in biases]
    for pair in range(heads // 2):
        both = slice(pair * wide, (pair + 1) * wide)
        scores = dot(keys[...], query_ref[both], 1, 1)
        prob_grad_ref[:, both] = dot(values[...], grad_ref[both], 1, 1)
        pieces = [scores[:rows], scores[rows:]]
        if is_own:
            pieces[1] = jnp.where(causal, pieces[1], NEG_FILL)
        tops = [jnp.max(piece, axis=0, keepdims=True) for piece in pieces]
        top = jnp.maximum(tops[0] + bias[0], tops[1] + bias[1])
        total = jnp.zeros_like(top)
        for i, piece in enumerate(pieces):
            power = jnp.exp2(piece * shade + (bias[i] - shade * top))
            total = total + jnp.sum(power, axis=0, keepdims=True)
            powers_ref[i * rows : (i + 1) * rows, both] = power.astype(BF16)
        stats_ref[0:1, both] = top
        stats_ref[1:2, both] = total


def scaled(ref, scales_ref, row):
    return (ref[...].astype(F32) * scales_ref[row : row + 1, :]).astype(BF16)


def store_grads(ref, score_grad, powers, query_t, grad_t, scaling):
    dim = query_t.shape[0]
    ref[:, :dim] = (dot(score_grad, query_t, 1, 1) * scaling).astype(ref.dtype)
    ref[:, dim:] = dot(powers, grad_t, 1, 1).astype(ref.dtype)


def late_kernel(
    facts_ref,
    query_ref,
    query_t_ref,
    grad_ref,
    grad_t_ref,
    own_powers,
    own_stats,
    own_values_t,
    near_powers,
    near_stats,
    near_values_t,
    mate_ref,
    back_ref,
    output_t_ref,
    score_grad,
    keys_t,
    scales_ref,
    keys,
    values,
    values_t,
    powers,
    prob_grad,
    stats,
):
    rows, dim = keys.shape[0] // 2, keys.shape[1]
    heads = query_ref.shape[0] // rows
    scaling = 1.0 / math.sqrt(dim)
    shade = LOG2_E * scaling
    load_blocks(((mate_ref, 0), (mate_ref, rows)), keys, values, keys_t, values_t)
    wide = 2 * rows
    spans = [slice(pair * wide, (pair + 1) * wide) for pair in range(heads // 2)]
    bias = [fact(facts_ref, row, wide) for row in (BIAS_MATE, BIAS_CROSS)]
    for both in spans:
        scores = dot(keys[...], query_ref[both], 1, 1)
        prob_grad[:, both] = dot(values[...], grad_ref[both], 1, 1)
        pieces = [scores[:rows], scores[rows:]]
        tops = [jnp.max(pieces[i], axis=0, keepdims=True) + bias[i] for i in (0, 1)]
        top = jnp.maximum(tops[0], tops[1])
        total = jnp.zeros_like(top)
        for i, piece in enumerate(pieces):
            power = jnp.exp2(piece * shade + (bias[i] - shade * top))
            total = total + jnp.sum(power, axis=0, keepdims=True)
            powers[i * rows : (i + 1) * rows, both] = power.astype(BF16)
        stats[0:1, both] = top
        stats[1:2, both] = total

    sets = (
        (own_powers, own_stats, own_values_t),
        (near_powers, near_stats, near_values_t),
        (powers, stats, values_t),
    )
    tops = [item[1][0:1, :] for item in sets]
    top = jnp.maximum(jnp.maximum(tops[0], tops[1]), tops[2])
    fades = [jnp.exp2((part - top) * shade) for part in tops]
    total = sum(item[1][1:2, :] * fade for item, fade in zip(sets, fades))
    inverse = 1.0 / total
    for i, fade in enumerate(fades):
        scales_ref[i : i + 1, :] = fade * inverse
    for both in spans:
        output_t = sum(
            dot(item[2][...], item[0][:, both], 1, 0) * scales_ref[i : i + 1, both]
            for i, item in enumerate(sets)
        )
        output_t_ref[:, both] = output_t
        delta = jnp.sum(grad_t_ref[:, both].astype(F32) * output_t, axis=0, keepdims=True)
        scales_ref[3:4, both] = delta
        score_grad[:, both] = (
            powers[:, both].astype(F32) * (prob_grad[:, both] - delta)
        ).astype(BF16)
    store_grads(
        back_ref,
        score_grad[...],
        powers[...],
        scaled(query_t_ref, scales_ref, 2),
        scaled(grad_t_ref, scales_ref, 2),
        scaling,
    )


def near_kernel(
    query_t_ref, grad_t_ref, powers, prob_grad, scales_ref, near_ref, score_grad
):
    scaling = 1.0 / math.sqrt(query_t_ref.shape[0])
    delta = scales_ref[3:4, :]
    score_grad[...] = (powers[...].astype(F32) * (prob_grad[...] - delta)).astype(BF16)
    store_grads(
        near_ref,
        score_grad[...],
        powers[...],
        scaled(query_t_ref, scales_ref, 1),
        scaled(grad_t_ref, scales_ref, 1),
        scaling,
    )


def query_kernel(
    facts_ref,
    query_t_ref,
    grad_t_ref,
    output_t_ref,
    scales_ref,
    own_powers,
    own_prob_grad,
    near_score_grad,
    mate_score_grad,
    own_keys_t,
    near_keys_t,
    mate_keys_t,
    attended_ref,
    query_grad_ref,
    back_ref,
    local_ref,
    own_score_grad,
    grads_ref,
):
    rows = attended_ref.shape[0]
    dim = output_t_ref.shape[0]
    scaling = 1.0 / math.sqrt(dim)
    wide = 2 * rows
    valid = fact(facts_ref, VALID, wide)
    for pair in range(output_t_ref.shape[1] // wide):
        both = slice(pair * wide, (pair + 1) * wide)
        delta = scales_ref[3:4, both]
        own_score_grad[:, both] = (
            own_powers[:, both].astype(F32) * (own_prob_grad[:, both] - delta)
        ).astype(BF16)
        sets = (
            (own_keys_t, own_score_grad),
            (near_keys_t, near_score_grad),
            (mate_keys_t, mate_score_grad),
        )
        grad_t = sum(
            dot(part_t[...], part[:, both], 1, 0) * scales_ref[i : i + 1, both]
            for i, (part_t, part) in enumerate(sets)
        )
        query_grad = (grad_t * scaling).T
        output = (output_t_ref[:, both] * valid).T
        for i in (0, 1):
            span = slice((2 * pair + i) * dim, (2 * pair + i + 1) * dim)
            part = slice(i * rows, (i + 1) * rows)
            attended_ref[:, span] = output[part].astype(BF16)
            query_grad_ref[:, span] = query_grad[part]
    store_grads(
        grads_ref,
        own_score_grad[...],
        own_powers[...],
        scaled(query_t_ref, scales_ref, 0),
        scaled(grad_t_ref, scales_ref, 0),
        scaling,
    )
    back_ref[...] = grads_ref[:rows].astype(BF16)
    local_ref[...] = grads_ref[rows:]


def merge_kernel(first_ref, back_ref, near_out, over_out):
    rows = first_ref.shape[0] // 2
    near_out[...] = (first_ref[:rows] + back_ref[:rows].astype(F32)).astype(BF16)
    over_out[...] = (first_ref[rows:] + back_ref[rows:].astype(F32)).astype(BF16)


def return_kernel(
    facts_ref, totals_ref, near_ref, group_ref, seq_ref, cross_ref, prompt_ref, pay6, pay5
):
    rows = prompt_ref.shape[0]
    sums = [ref[...].astype(F32) for ref in (near_ref, group_ref, seq_ref, cross_ref)]
    prompt_ref[...] = (sums[0] + sums[2]) * fact(facts_ref, IS_PROMPT)
    for ref, base in ((pay6, FROM6), (pay5, FROM5)):
        total = sum(part * fact(facts_ref, base + i) for i, part in enumerate(sums))
        ref[:rows] = total.astype(BF16)
        store_tail(ref, rows, totals_ref[...])


def finish_kernel(
    facts_ref,
    local_ref,
    mate_ref,
    prompt_ref,
    far5,
    far6,
    totals_ref,
    rest_ref,
    query_part_ref,
    query_grad_ref,
    key_grad_ref,
    value_grad_ref,
    loss_ref,
):
    rows, dim = key_grad_ref.shape
    totals = (totals_ref[...] + rest_ref[...]) + (decode(far6, rows) + decode(far5, rows))
    margin = totals - jnp.concatenate([totals[1:], totals[:1]], axis=0)
    slope = -BETA * margin
    small = jnp.exp(-jnp.abs(slope))
    bigger = 1.0 + small
    gap = bigger - 1.0
    log_part = jnp.where(
        gap == 0.0, small, jnp.log(bigger) * (small / jnp.where(gap == 0.0, 1.0, gap))
    )
    loss = jnp.maximum(slope, 0.0) + log_part
    weight = jnp.where(slope >= 0.0, 1.0, small) / bigger
    row = lax.broadcasted_iota(jnp.int32, (8, 128), 0)
    lane = lax.broadcasted_iota(jnp.int32, (8, 128), 1)
    in_lanes = jnp.sum(jnp.where(row == 2 * lane, loss, 0.0), axis=0, keepdims=True)
    loss_ref[...] = in_lanes[:, : loss_ref.shape[1]]
    mine = row.astype(F32) == fact(facts_ref, PAIR_ROW, 128)
    scale = jnp.sum(jnp.where(mine, weight, 0.0), axis=0, keepdims=True)
    far_sum = far6[:rows].astype(F32) + far5[:rows].astype(F32)
    total = local_ref[...] + mate_ref[...].astype(F32) + prompt_ref[...]
    total = total + far_sum * fact(facts_ref, IS_PROMPT)
    key_grad_ref[...] = (total[:, :dim] * scale).astype(BF16)
    value_grad_ref[...] = (total[:, dim:] * scale).astype(BF16)
    for start in range(0, query_grad_ref.shape[1], dim):
        span = slice(start, start + dim)
        query_grad_ref[:, span] = (query_part_ref[:, span] * scale).astype(BF16)


def call(kernel, out_shapes, operands, scratch=(), in_hbm=0, flops=0):
    single = not isinstance(out_shapes, (list, tuple))
    plain = len(operands) - in_hbm
    held = [
        pltpu.with_memory_space_constraint(operand, pltpu.HBM) for operand in operands[plain:]
    ]
    return pl.pallas_call(
        kernel,
        out_shape=out_shapes,
        in_specs=[VMEM_SPEC] * plain + [HBM_SPEC] * in_hbm,
        out_specs=VMEM_SPEC if single else [VMEM_SPEC] * len(out_shapes),
        scratch_shapes=list(scratch),
        compiler_params=pltpu.CompilerParams(vmem_limit_bytes=VMEM_BYTES),
        cost_estimate=pl.CostEstimate(flops=flops, bytes_accessed=0, transcendentals=0),
    )(*operands[:plain], *held)


def swap(count, turn):
    return [(i, i ^ turn) for i in range(count)]


def body(
    queries, key_heads, value_heads, cotangent, loss_mask, log_ratio, block_counts, response_order
):
    seq_count = lax.axis_size("seq")
    group_count = lax.axis_size("grp")
    head_count = lax.axis_size("head")
    rows = queries.shape[1]
    dim = key_heads.shape[2]
    width = queries.shape[2]
    heads = width // dim
    both = 2 * dim
    every = heads * rows
    shape = jax.ShapeDtypeStruct
    dma = pltpu.SemaphoreType.DMA
    tie = lax.optimization_barrier
    packed = shape((rows + TAIL, both), BF16)
    total_tile = shape((8, 128), F32)
    grads = shape((rows, both), BF16)
    grads_wide = shape((rows, both), F32)

    def along_grp(value, turn):
        return lax.ppermute(value, "grp", swap(group_count, turn))

    def along_seq(value, turn):
        return lax.ppermute(value, "seq", swap(seq_count, turn))

    def across(value):
        turns = [
            (s * group_count + g, (s ^ 2) * group_count + (g ^ 1))
            for s in range(seq_count)
            for g in range(group_count)
        ]
        return lax.ppermute(value, ("seq", "grp"), turns)

    def along_x(value, step):
        near = [(h, h ^ 2) for h in range(head_count)]
        round_way = [(h, (3 - h // 2) * 2 + h % 2) for h in range(head_count)]
        return lax.ppermute(value, "head", round_way if step else near)

    def along_y(value):
        return lax.ppermute(value, "head", swap(head_count, 1))

    own = call(
        pack_kernel, grads, (key_heads[0], value_heads[0]), scratch=[dma((2,))], in_hbm=2
    )
    far6 = along_grp(own, 6)
    far5 = along_grp(own, 5)
    own, response_order = tie((own, response_order))
    facts, totals, kept = call(
        facts_kernel,
        [shape((FACTS, both), F32), total_tile, shape((1, rows), F32)],
        (response_order, block_counts, loss_mask, log_ratio),
        scratch=[
            pltpu.SMEM(response_order.shape, jnp.int32),
            pltpu.SMEM(block_counts.shape, jnp.int32),
            pltpu.VMEM(loss_mask.shape, jnp.int32),
            pltpu.VMEM(log_ratio.shape, F32),
            dma((4,)),
        ],
        in_hbm=4,
    )
    mate_own = along_seq(own, 1)
    stacked = shape((every, dim), BF16)
    query_rows, query_cols, grad_rows, grad_cols = call(
        prepare_kernel,
        [stacked, shape((dim, every), BF16), stacked, shape((dim, every), BF16)],
        (kept, queries[0], cotangent[0]),
        scratch=[pltpu.VMEM((every, dim), BF16), dma((2, heads))],
        in_hbm=2,
    )
    part = along_y(totals)
    far6, far5, totals, query_rows = tie((far6, far5, totals, query_rows))
    totals = totals + part
    far6, far5, totals = tie((far6, far5, totals))
    to_group, to_seq, to_cross = call(
        route_kernel, [packed] * 3, (facts, totals, own, far6, far5)
    )
    from_seq = along_seq(to_seq, 2)
    from_group = along_grp(to_group, 1)
    from_cross = across(to_cross)

    def early(biases, is_own, left, right):
        return call(
            functools.partial(early_kernel, biases, is_own),
            [
                shape((2 * rows, every), BF16),
                shape((2 * rows, every), F32),
                shape((8, every), F32),
                shape((dim, 2 * rows), BF16),
                shape((dim, 2 * rows), BF16),
            ],
            (facts, query_rows, grad_rows, left, right),
            scratch=[pltpu.VMEM((2 * rows, dim), BF16)] * 2,
            flops=8 * rows * every * dim,
        )

    own_set = early((BIAS_OWN, None), True, mate_own, own)
    from_cross, own_powers = tie((from_cross, own_set[0]))
    near, totals = call(
        select_kernel,
        [shape((2 * rows, both), BF16), shape((rows, 128), F32)],
        (facts, totals, own, far6, far5, from_group, from_seq, from_cross),
    )
    mate = along_seq(near, 1)
    near_set = early((BIAS_FIRST, BIAS_OVER), False, near, near)
    part = along_seq(totals, 1)
    mate, near_powers = tie((mate, near_set[0]))
    back, output_t, mate_sg, mate_keys_t, scales = call(
        late_kernel,
        [
            shape((2 * rows, both), BF16),
            shape((dim, every), F32),
            shape((2 * rows, every), BF16),
            shape((dim, 2 * rows), BF16),
            shape((8, every), F32),
        ],
        (
            facts,
            query_rows,
            query_cols,
            grad_rows,
            grad_cols,
            own_powers,
            own_set[2],
            own_set[4],
            near_powers,
            near_set[2],
            near_set[4],
            mate,
        ),
        scratch=[
            pltpu.VMEM((2 * rows, dim), BF16),
            pltpu.VMEM((2 * rows, dim), BF16),
            pltpu.VMEM((dim, 2 * rows), BF16),
            pltpu.VMEM((2 * rows, every), BF16),
            pltpu.VMEM((2 * rows, every), F32),
            pltpu.VMEM((8, every), F32),
        ],
        flops=24 * rows * every * dim,
    )
    back, totals = tie((back, totals))
    back, totals = tie((back, totals + part))
    back = along_seq(back, 1)
    part = along_x(totals, 0)
    first, near_sg = call(
        near_kernel,
        [shape((2 * rows, both), F32), shape((2 * rows, every), BF16)],
        (query_cols, grad_cols, near_powers, near_set[1], scales),
        flops=8 * rows * every * dim,
    )
    near_sum, over_sum = call(merge_kernel, [grads, grads], (first, back))
    from_seq = along_seq(over_sum, 2)
    from_group = along_grp(near_sum, 1)
    from_cross = across(over_sum)
    totals = (totals + part)[:8]
    totals = totals + along_x(totals, 1)
    attended, query_part, own_back, local = call(
        query_kernel,
        [shape((rows, width), BF16), shape((rows, width), F32), grads, grads_wide],
        (
            facts,
            query_cols,
            grad_cols,
            output_t,
            scales,
            own_powers,
            own_set[1],
            near_sg,
            mate_sg,
            own_set[3],
            near_set[3],
            mate_keys_t,
        ),
        scratch=[
            pltpu.VMEM((2 * rows, every), BF16),
            pltpu.VMEM((2 * rows, both), F32),
        ],
        flops=20 * rows * every * dim,
    )
    from_cross, query_part = tie((from_cross, query_part))
    from_prompt, pay6, pay5 = call(
        return_kernel,
        [grads_wide, packed, packed],
        (facts, totals, near_sum, from_group, from_seq, from_cross),
    )
    far5 = along_grp(pay5, 5)
    far6 = along_grp(pay6, 6)
    own_back = along_seq(own_back, 1)
    rest = along_grp(totals, 2)
    query_grad, key_grad, value_grad, loss = call(
        finish_kernel,
        [
            shape((rows, width), BF16),
            shape((rows, dim), BF16),
            shape((rows, dim), BF16),
            shape((1, group_count // 2), F32),
        ],
        (facts, local, own_back, from_prompt, far5, far6, totals, rest, query_part),
    )
    return attended[None], query_grad[None], key_grad[None], value_grad[None], loss[0]


def solution(mesh):
    spec = P("grp", "seq", "head")
    in_specs = (spec, spec, spec, spec, P("grp", "seq"), P("grp", ("seq", "head")), P(), P())
    out_specs = (spec, spec, spec, spec, P())
    return jax.shard_map(body, mesh=mesh, in_specs=in_specs, out_specs=out_specs, check_vma=False)
```

```python
import functools
import math

import jax
import jax.numpy as jnp
from jax import lax
from jax.experimental import pallas as pl
from jax.experimental.pallas import tpu as pltpu
from jax.sharding import PartitionSpec as P

LEN_BLOCK = 128
BETA = 0.1
NEG_FILL = -1e30
LOG2_E = math.log2(math.e)
TAIL = 16
F32 = jnp.float32
BF16 = jnp.bfloat16
VMEM_BYTES = 40 * 1024 * 1024

VMEM_SPEC = pl.BlockSpec(memory_space=pltpu.VMEM)
HBM_SPEC = pl.BlockSpec(memory_space=pltpu.HBM)

FROM6, FROM5, IS_PROMPT, VALID, PAIR_ROW = 0, 4, 8, 9, 10
BIAS_FIRST, BIAS_MATE, BIAS_OVER, BIAS_CROSS, BIAS_OWN = 11, 12, 13, 14, 15
FACTS = 16


def dot(lhs, rhs, lhs_dim, rhs_dim):
    return lax.dot_general(
        lhs, rhs, (((lhs_dim,), (rhs_dim,)), ((), ())), preferred_element_type=F32
    )


def fact(facts_ref, row, width=None):
    return facts_ref[row : row + 1, :width]


def store_tail(ref, row, totals):
    high = totals.astype(BF16).astype(F32)
    rest = totals - high
    middle = rest.astype(BF16).astype(F32)
    low = rest - middle
    zero = jnp.zeros_like(middle)
    ref[row : row + TAIL, :128] = jnp.concatenate([high, low], axis=0).astype(BF16)
    ref[row : row + TAIL, 128:] = jnp.concatenate([middle, zero], axis=0).astype(BF16)


def decode(ref, row):
    left = ref[row : row + TAIL, :128].astype(F32)
    right = ref[row : row + TAIL, 128:].astype(F32)
    return (left[:8] + right[:8]) + left[8:]


def facts_kernel(
    order_hbm,
    counts_hbm,
    mask_hbm,
    ratio_hbm,
    key_hbm,
    value_hbm,
    own_ref,
    facts_ref,
    totals_ref,
    kept_ref,
    order_ref,
    counts_ref,
    mask_ref,
    ratio_ref,
    sems,
):
    dim = key_hbm.shape[1]
    copies = [
        pltpu.make_async_copy(source, target, sems.at[i])
        for i, (source, target) in enumerate(
            (
                (order_hbm, order_ref),
                (counts_hbm, counts_ref),
                (mask_hbm, mask_ref),
                (ratio_hbm, ratio_ref),
                (key_hbm, own_ref.at[:, pl.ds(0, dim)]),
                (value_hbm, own_ref.at[:, pl.ds(dim, dim)]),
            )
        )
    ]
    for copy in copies:
        copy.start()
    seq = lax.axis_index("seq")
    grp = lax.axis_index("grp")
    head = lax.axis_index("head")
    pairs = lax.axis_size("grp") // 2
    is_response = grp >= pairs
    for copy in copies[:4]:
        copy.wait()

    def pair_of(group, half):
        return order_ref[jnp.where(is_response, 2 * (group - pairs), 0) + half] // 2

    def put(row, value):
        facts_ref[row : row + 1, :] = jnp.full((1, facts_ref.shape[1]), value, F32)

    def flag(row, condition, yes=1.0, no=0.0):
        put(row, jnp.where(condition, yes, no).astype(F32))

    half = seq // 2
    slots = [pair_of(group, side) for side in (half, 1 - half) for group in (grp, grp ^ 1)]
    for number, pair in enumerate(slots):
        flag(FROM6 + number, jnp.logical_and(is_response, pair == (grp ^ 6)))
        flag(FROM5 + number, jnp.logical_and(is_response, pair == (grp ^ 5)))
    slot = jnp.where(is_response, 2 * (grp - pairs), 0) + half
    filled = seq % 2 < counts_ref[slot]
    valid = jnp.logical_or(jnp.logical_not(is_response), filled)
    my_pair = jnp.where(is_response, order_ref[slot] // 2, jnp.minimum(grp, pairs - 1))
    flag(IS_PROMPT, jnp.logical_not(is_response))
    flag(VALID, valid)
    put(PAIR_ROW, (2 * my_pair).astype(F32))
    flag(BIAS_FIRST, is_response, 0.0, NEG_FILL)
    flag(BIAS_MATE, jnp.logical_or(is_response, seq % 2 == 1), 0.0, NEG_FILL)
    flag(BIAS_OVER, jnp.logical_or(is_response, seq >= 2), 0.0, NEG_FILL)
    flag(BIAS_CROSS, jnp.logical_or(is_response, seq >= 2), 0.0, NEG_FILL)
    flag(BIAS_OWN, jnp.logical_and(is_response, seq % 2 == 1), 0.0, NEG_FILL)

    piece = ratio_ref.shape[1]
    lane = lax.broadcasted_iota(jnp.int32, (piece, 128), 1)
    spot = lax.broadcasted_iota(jnp.int32, (piece, 128), 0)
    place_at = (lane == spot + head * piece).astype(F32)
    spread = lax.dot_general(
        jnp.broadcast_to(ratio_ref[...], (8, piece)),
        place_at,
        (((1,), (0,)), ((), ())),
        precision=lax.Precision.HIGHEST,
        preferred_element_type=F32,
    )
    kept = mask_ref[...] > 0
    partial = jnp.sum(jnp.where(kept, spread[:1], 0.0), axis=1, keepdims=True)
    row = lax.broadcasted_iota(jnp.int32, (8, 128), 0)
    mine = jnp.where(jnp.logical_and(is_response, filled), order_ref[slot], -1)
    totals_ref[...] = jnp.where(row == mine, jnp.broadcast_to(partial, (8, 128)), 0.0)
    negative = jnp.logical_and(is_response, order_ref[slot] % 2 == 0)
    sign = jnp.where(valid, jnp.where(negative, -1.0, 1.0), 0.0).astype(F32)
    kept_ref[...] = jnp.where(kept, sign, 0.0)
    for copy in copies[4:]:
        copy.wait()


def prepare_kernel(
    kept_ref, query_hbm, cot_hbm, query_ref, query_t_ref, grad_ref, grad_t_ref, cots, sems
):
    rows = kept_ref.shape[1]
    dim = query_ref.shape[1]
    heads = query_ref.shape[0] // rows
    copies = []
    for i in range(heads):
        for j, (source, target) in enumerate(((cot_hbm, cots), (query_hbm, query_ref))):
            copies.append(
                pltpu.make_async_copy(
                    source.at[:, pl.ds(i * dim, dim)],
                    target.at[pl.ds(i * rows, rows)],
                    sems.at[j, i],
                )
            )
    for copy in copies:
        copy.start()
    kept_rows = jnp.broadcast_to(kept_ref[...], (rows, rows)).T
    for copy in copies:
        copy.wait()
    for i in range(heads):
        part = slice(i * rows, (i + 1) * rows)
        grad = (cots[part].astype(F32) * kept_rows).astype(BF16)
        grad_ref[part] = grad
        grad_t_ref[:, part] = grad.T
        query_t_ref[:, part] = query_ref[part].T


def route_kernel(facts_ref, totals_ref, own_ref, far6, far5, group_ref, seq_ref, cross_ref):
    rows = own_ref.shape[0]
    for number, ref in ((1, group_ref), (2, seq_ref), (3, cross_ref)):
        picked = far6[...].astype(F32) * fact(facts_ref, FROM6 + number)
        picked = picked + far5[...].astype(F32) * fact(facts_ref, FROM5 + number)
        if number == 2:
            picked = picked + own_ref[...].astype(F32) * fact(facts_ref, IS_PROMPT)
        ref[:rows] = picked.astype(BF16)
        store_tail(ref, rows, totals_ref[...])


def select_kernel(
    facts_ref, totals_ref, own_ref, far6, far5, group_ref, seq_ref, cross_ref, near_ref, sum_ref
):
    rows = own_ref.shape[0]
    first = far6[...].astype(F32) * fact(facts_ref, FROM6)
    first = first + far5[...].astype(F32) * fact(facts_ref, FROM5)
    first = first + own_ref[...].astype(F32) * fact(facts_ref, IS_PROMPT)
    near_ref[:rows] = (first + group_ref[:rows].astype(F32)).astype(BF16)
    near_ref[rows:] = (seq_ref[:rows].astype(F32) + cross_ref[:rows].astype(F32)).astype(BF16)
    totals = (totals_ref[...] + decode(group_ref, rows)) + (
        decode(seq_ref, rows) + decode(cross_ref, rows)
    )
    sum_ref[...] = jnp.concatenate([totals] * (sum_ref.shape[0] // 8), axis=0)


def load_blocks(blocks, keys, values, keys_t, values_t):
    dim = keys.shape[1]
    rows = keys.shape[0] // len(blocks)
    for number, (ref, start) in enumerate(blocks):
        part = slice(number * rows, (number + 1) * rows)
        key_part = ref[start : start + rows, :dim]
        value_part = ref[start : start + rows, dim:]
        keys[part] = key_part
        values[part] = value_part
        keys_t[:, part] = key_part.T
        values_t[:, part] = value_part.T


def early_kernel(
    biases,
    is_own,
    facts_ref,
    query_ref,
    grad_ref,
    left_ref,
    right_ref,
    powers_ref,
    prob_grad_ref,
    stats_ref,
    keys_t,
    values_t,
    keys,
    values,
):
    rows = keys.shape[0] // 2
    heads = query_ref.shape[0] // rows
    shade = LOG2_E / math.sqrt(keys.shape[1])
    start = 0 if is_own else rows
    load_blocks(((left_ref, 0), (right_ref, start)), keys, values, keys_t, values_t)
    wide = 2 * rows
    key_id = lax.broadcasted_iota(jnp.int32, (rows, wide), 0)
    row_id = lax.broadcasted_iota(jnp.int32, (rows, wide), 1) % rows
    causal = key_id <= row_id
    bias = [fact(facts_ref, row, wide) if row is not None else 0.0 for row in biases]
    for pair in range(heads // 2):
        both = slice(pair * wide, (pair + 1) * wide)
        scores = dot(keys[...], query_ref[both], 1, 1)
        prob_grad_ref[:, both] = dot(values[...], grad_ref[both], 1, 1)
        pieces = [scores[:rows], scores[rows:]]
        if is_own:
            pieces[1] = jnp.where(causal, pieces[1], NEG_FILL)
        tops = [jnp.max(piece, axis=0, keepdims=True) for piece in pieces]
        top = jnp.maximum(tops[0] + bias[0], tops[1] + bias[1])
        total = jnp.zeros_like(top)
        for i, piece in enumerate(pieces):
            power = jnp.exp2(piece * shade + (bias[i] - shade * top))
            total = total + jnp.sum(power, axis=0, keepdims=True)
            powers_ref[i * rows : (i + 1) * rows, both] = power.astype(BF16)
        stats_ref[0:1, both] = top
        stats_ref[1:2, both] = total


def scaled(ref, scales_ref, row):
    return (ref[...].astype(F32) * scales_ref[row : row + 1, :]).astype(BF16)


def store_grads(ref, score_grad, powers, query_t, grad_t, scaling):
    dim = query_t.shape[0]
    ref[:, :dim] = (dot(score_grad, query_t, 1, 1) * scaling).astype(ref.dtype)
    ref[:, dim:] = dot(powers, grad_t, 1, 1).astype(ref.dtype)


def late_kernel(
    facts_ref,
    query_ref,
    query_t_ref,
    grad_ref,
    grad_t_ref,
    own_powers,
    own_stats,
    own_values_t,
    near_powers,
    near_stats,
    near_values_t,
    mate_ref,
    back_ref,
    output_t_ref,
    score_grad,
    keys_t,
    scales_ref,
    keys,
    values,
    values_t,
    powers,
    prob_grad,
    stats,
):
    rows, dim = keys.shape[0] // 2, keys.shape[1]
    heads = query_ref.shape[0] // rows
    scaling = 1.0 / math.sqrt(dim)
    shade = LOG2_E * scaling
    load_blocks(((mate_ref, 0), (mate_ref, rows)), keys, values, keys_t, values_t)
    wide = 2 * rows
    spans = [slice(pair * wide, (pair + 1) * wide) for pair in range(heads // 2)]
    bias = [fact(facts_ref, row, wide) for row in (BIAS_MATE, BIAS_CROSS)]
    for both in spans:
        scores = dot(keys[...], query_ref[both], 1, 1)
        prob_grad[:, both] = dot(values[...], grad_ref[both], 1, 1)
        pieces = [scores[:rows], scores[rows:]]
        tops = [jnp.max(pieces[i], axis=0, keepdims=True) + bias[i] for i in (0, 1)]
        top = jnp.maximum(tops[0], tops[1])
        total = jnp.zeros_like(top)
        for i, piece in enumerate(pieces):
            power = jnp.exp2(piece * shade + (bias[i] - shade * top))
            total = total + jnp.sum(power, axis=0, keepdims=True)
            powers[i * rows : (i + 1) * rows, both] = power.astype(BF16)
        stats[0:1, both] = top
        stats[1:2, both] = total

    sets = (
        (own_powers, own_stats, own_values_t),
        (near_powers, near_stats, near_values_t),
        (powers, stats, values_t),
    )
    tops = [item[1][0:1, :] for item in sets]
    top = jnp.maximum(jnp.maximum(tops[0], tops[1]), tops[2])
    fades = [jnp.exp2((part - top) * shade) for part in tops]
    total = sum(item[1][1:2, :] * fade for item, fade in zip(sets, fades))
    inverse = 1.0 / total
    for i, fade in enumerate(fades):
        scales_ref[i : i + 1, :] = fade * inverse
    for both in spans:
        output_t = sum(
            dot(item[2][...], item[0][:, both], 1, 0) * scales_ref[i : i + 1, both]
            for i, item in enumerate(sets)
        )
        output_t_ref[:, both] = output_t
        delta = jnp.sum(grad_t_ref[:, both].astype(F32) * output_t, axis=0, keepdims=True)
        scales_ref[3:4, both] = delta
        score_grad[:, both] = (
            powers[:, both].astype(F32) * (prob_grad[:, both] - delta)
        ).astype(BF16)
    store_grads(
        back_ref,
        score_grad[...],
        powers[...],
        scaled(query_t_ref, scales_ref, 2),
        scaled(grad_t_ref, scales_ref, 2),
        scaling,
    )


def near_kernel(
    query_t_ref, grad_t_ref, powers, prob_grad, scales_ref, near_ref, score_grad
):
    scaling = 1.0 / math.sqrt(query_t_ref.shape[0])
    delta = scales_ref[3:4, :]
    score_grad[...] = (powers[...].astype(F32) * (prob_grad[...] - delta)).astype(BF16)
    store_grads(
        near_ref,
        score_grad[...],
        powers[...],
        scaled(query_t_ref, scales_ref, 1),
        scaled(grad_t_ref, scales_ref, 1),
        scaling,
    )


def query_kernel(
    facts_ref,
    query_t_ref,
    grad_t_ref,
    output_t_ref,
    scales_ref,
    own_powers,
    own_prob_grad,
    near_score_grad,
    mate_score_grad,
    own_keys_t,
    near_keys_t,
    mate_keys_t,
    attended_ref,
    query_grad_ref,
    back_ref,
    local_ref,
    own_score_grad,
    grads_ref,
):
    rows = attended_ref.shape[0]
    dim = output_t_ref.shape[0]
    scaling = 1.0 / math.sqrt(dim)
    wide = 2 * rows
    valid = fact(facts_ref, VALID, wide)
    for pair in range(output_t_ref.shape[1] // wide):
        both = slice(pair * wide, (pair + 1) * wide)
        delta = scales_ref[3:4, both]
        own_score_grad[:, both] = (
            own_powers[:, both].astype(F32) * (own_prob_grad[:, both] - delta)
        ).astype(BF16)
        sets = (
            (own_keys_t, own_score_grad),
            (near_keys_t, near_score_grad),
            (mate_keys_t, mate_score_grad),
        )
        grad_t = sum(
            dot(part_t[...], part[:, both], 1, 0) * scales_ref[i : i + 1, both]
            for i, (part_t, part) in enumerate(sets)
        )
        query_grad = (grad_t * scaling).T
        output = (output_t_ref[:, both] * valid).T
        for i in (0, 1):
            span = slice((2 * pair + i) * dim, (2 * pair + i + 1) * dim)
            part = slice(i * rows, (i + 1) * rows)
            attended_ref[:, span] = output[part].astype(BF16)
            query_grad_ref[:, span] = query_grad[part]
    store_grads(
        grads_ref,
        own_score_grad[...],
        own_powers[...],
        scaled(query_t_ref, scales_ref, 0),
        scaled(grad_t_ref, scales_ref, 0),
        scaling,
    )
    back_ref[...] = grads_ref[:rows].astype(BF16)
    local_ref[...] = grads_ref[rows:]


def merge_kernel(first_ref, back_ref, near_out, over_out):
    rows = first_ref.shape[0] // 2
    near_out[...] = (first_ref[:rows] + back_ref[:rows].astype(F32)).astype(BF16)
    over_out[...] = (first_ref[rows:] + back_ref[rows:].astype(F32)).astype(BF16)


def return_kernel(
    facts_ref, totals_ref, near_ref, group_ref, seq_ref, cross_ref, prompt_ref, pay6, pay5
):
    rows = prompt_ref.shape[0]
    sums = [ref[...].astype(F32) for ref in (near_ref, group_ref, seq_ref, cross_ref)]
    prompt_ref[...] = (sums[0] + sums[2]) * fact(facts_ref, IS_PROMPT)
    for ref, base in ((pay6, FROM6), (pay5, FROM5)):
        total = sum(part * fact(facts_ref, base + i) for i, part in enumerate(sums))
        ref[:rows] = total.astype(BF16)
        store_tail(ref, rows, totals_ref[...])


def finish_kernel(
    facts_ref,
    local_ref,
    mate_ref,
    prompt_ref,
    far5,
    far6,
    totals_ref,
    rest_ref,
    query_part_ref,
    query_grad_ref,
    key_grad_ref,
    value_grad_ref,
    loss_ref,
):
    rows, dim = key_grad_ref.shape
    totals = (totals_ref[...] + rest_ref[...]) + (decode(far6, rows) + decode(far5, rows))
    margin = totals - jnp.concatenate([totals[1:], totals[:1]], axis=0)
    slope = -BETA * margin
    small = jnp.exp(-jnp.abs(slope))
    bigger = 1.0 + small
    gap = bigger - 1.0
    log_part = jnp.where(
        gap == 0.0, small, jnp.log(bigger) * (small / jnp.where(gap == 0.0, 1.0, gap))
    )
    loss = jnp.maximum(slope, 0.0) + log_part
    weight = jnp.where(slope >= 0.0, 1.0, small) / bigger
    row = lax.broadcasted_iota(jnp.int32, (8, 128), 0)
    lane = lax.broadcasted_iota(jnp.int32, (8, 128), 1)
    in_lanes = jnp.sum(jnp.where(row == 2 * lane, loss, 0.0), axis=0, keepdims=True)
    loss_ref[...] = in_lanes[:, : loss_ref.shape[1]]
    mine = row.astype(F32) == fact(facts_ref, PAIR_ROW, 128)
    scale = jnp.sum(jnp.where(mine, weight, 0.0), axis=0, keepdims=True)
    far_sum = far6[:rows].astype(F32) + far5[:rows].astype(F32)
    total = local_ref[...] + mate_ref[...].astype(F32) + prompt_ref[...]
    total = total + far_sum * fact(facts_ref, IS_PROMPT)
    key_grad_ref[...] = (total[:, :dim] * scale).astype(BF16)
    value_grad_ref[...] = (total[:, dim:] * scale).astype(BF16)
    for start in range(0, query_grad_ref.shape[1], dim):
        span = slice(start, start + dim)
        query_grad_ref[:, span] = (query_part_ref[:, span] * scale).astype(BF16)


def call(kernel, out_shapes, operands, scratch=(), in_hbm=0, flops=0):
    single = not isinstance(out_shapes, (list, tuple))
    plain = len(operands) - in_hbm
    held = [
        pltpu.with_memory_space_constraint(operand, pltpu.HBM) for operand in operands[plain:]
    ]
    return pl.pallas_call(
        kernel,
        out_shape=out_shapes,
        in_specs=[VMEM_SPEC] * plain + [HBM_SPEC] * in_hbm,
        out_specs=VMEM_SPEC if single else [VMEM_SPEC] * len(out_shapes),
        scratch_shapes=list(scratch),
        compiler_params=pltpu.CompilerParams(vmem_limit_bytes=VMEM_BYTES),
        cost_estimate=pl.CostEstimate(flops=flops, bytes_accessed=0, transcendentals=0),
    )(*operands[:plain], *held)


def swap(count, turn):
    return [(i, i ^ turn) for i in range(count)]


def body(
    queries, key_heads, value_heads, cotangent, loss_mask, log_ratio, block_counts, response_order
):
    seq_count = lax.axis_size("seq")
    group_count = lax.axis_size("grp")
    head_count = lax.axis_size("head")
    rows = queries.shape[1]
    dim = key_heads.shape[2]
    width = queries.shape[2]
    heads = width // dim
    both = 2 * dim
    every = heads * rows
    shape = jax.ShapeDtypeStruct
    dma = pltpu.SemaphoreType.DMA
    tie = lax.optimization_barrier
    packed = shape((rows + TAIL, both), BF16)
    total_tile = shape((8, 128), F32)
    grads = shape((rows, both), BF16)
    grads_wide = shape((rows, both), F32)

    def along_grp(value, turn):
        return lax.ppermute(value, "grp", swap(group_count, turn))

    def along_seq(value, turn):
        return lax.ppermute(value, "seq", swap(seq_count, turn))

    def across(value):
        turns = [
            (s * group_count + g, (s ^ 2) * group_count + (g ^ 1))
            for s in range(seq_count)
            for g in range(group_count)
        ]
        return lax.ppermute(value, ("seq", "grp"), turns)

    def along_x(value, step):
        near = [(h, h ^ 2) for h in range(head_count)]
        round_way = [(h, (3 - h // 2) * 2 + h % 2) for h in range(head_count)]
        return lax.ppermute(value, "head", round_way if step else near)

    def along_y(value):
        return lax.ppermute(value, "head", swap(head_count, 1))

    own, facts, totals, kept = call(
        facts_kernel,
        [grads, shape((FACTS, both), F32), total_tile, shape((1, rows), F32)],
        (
            response_order,
            block_counts,
            loss_mask,
            log_ratio,
            key_heads[0],
            value_heads[0],
        ),
        scratch=[
            pltpu.SMEM(response_order.shape, jnp.int32),
            pltpu.SMEM(block_counts.shape, jnp.int32),
            pltpu.VMEM(loss_mask.shape, jnp.int32),
            pltpu.VMEM(log_ratio.shape, F32),
            dma((6,)),
        ],
        in_hbm=6,
    )
    far6 = along_grp(own, 6)
    far5 = along_grp(own, 5)
    mate_own = along_seq(own, 1)
    stacked = shape((every, dim), BF16)
    query_rows, query_cols, grad_rows, grad_cols = call(
        prepare_kernel,
        [stacked, shape((dim, every), BF16), stacked, shape((dim, every), BF16)],
        (kept, queries[0], cotangent[0]),
        scratch=[pltpu.VMEM((every, dim), BF16), dma((2, heads))],
        in_hbm=2,
    )
    part = along_y(totals)
    far6, far5, totals, query_rows = tie((far6, far5, totals, query_rows))
    totals = totals + part
    far6, far5, totals = tie((far6, far5, totals))
    to_group, to_seq, to_cross = call(
        route_kernel, [packed] * 3, (facts, totals, own, far6, far5)
    )
    from_seq = along_seq(to_seq, 2)
    from_group = along_grp(to_group, 1)
    from_cross = across(to_cross)

    def early(biases, is_own, left, right):
        return call(
            functools.partial(early_kernel, biases, is_own),
            [
                shape((2 * rows, every), BF16),
                shape((2 * rows, every), F32),
                shape((8, every), F32),
                shape((dim, 2 * rows), BF16),
                shape((dim, 2 * rows), BF16),
            ],
            (facts, query_rows, grad_rows, left, right),
            scratch=[pltpu.VMEM((2 * rows, dim), BF16)] * 2,
            flops=8 * rows * every * dim,
        )

    own_set = early((BIAS_OWN, None), True, mate_own, own)
    from_cross, own_powers = tie((from_cross, own_set[0]))
    near, totals = call(
        select_kernel,
        [shape((2 * rows, both), BF16), shape((rows, 128), F32)],
        (facts, totals, own, far6, far5, from_group, from_seq, from_cross),
    )
    mate = along_seq(near, 1)
    near_set = early((BIAS_FIRST, BIAS_OVER), False, near, near)
    part = along_seq(totals, 1)
    mate, near_powers = tie((mate, near_set[0]))
    back, output_t, mate_sg, mate_keys_t, scales = call(
        late_kernel,
        [
            shape((2 * rows, both), BF16),
            shape((dim, every), F32),
            shape((2 * rows, every), BF16),
            shape((dim, 2 * rows), BF16),
            shape((8, every), F32),
        ],
        (
            facts,
            query_rows,
            query_cols,
            grad_rows,
            grad_cols,
            own_powers,
            own_set[2],
            own_set[4],
            near_powers,
            near_set[2],
            near_set[4],
            mate,
        ),
        scratch=[
            pltpu.VMEM((2 * rows, dim), BF16),
            pltpu.VMEM((2 * rows, dim), BF16),
            pltpu.VMEM((dim, 2 * rows), BF16),
            pltpu.VMEM((2 * rows, every), BF16),
            pltpu.VMEM((2 * rows, every), F32),
            pltpu.VMEM((8, every), F32),
        ],
        flops=24 * rows * every * dim,
    )
    back, totals = tie((back, totals))
    back, totals = tie((back, totals + part))
    back = along_seq(back, 1)
    part = along_x(totals, 0)
    first, near_sg = call(
        near_kernel,
        [shape((2 * rows, both), F32), shape((2 * rows, every), BF16)],
        (query_cols, grad_cols, near_powers, near_set[1], scales),
        flops=8 * rows * every * dim,
    )
    near_sum, over_sum = call(merge_kernel, [grads, grads], (first, back))
    from_seq = along_seq(over_sum, 2)
    from_group = along_grp(near_sum, 1)
    from_cross = across(over_sum)
    totals = (totals + part)[:8]
    totals = totals + along_x(totals, 1)
    attended, query_part, own_back, local = call(
        query_kernel,
        [shape((rows, width), BF16), shape((rows, width), F32), grads, grads_wide],
        (
            facts,
            query_cols,
            grad_cols,
            output_t,
            scales,
            own_powers,
            own_set[1],
            near_sg,
            mate_sg,
            own_set[3],
            near_set[3],
            mate_keys_t,
        ),
        scratch=[
            pltpu.VMEM((2 * rows, every), BF16),
            pltpu.VMEM((2 * rows, both), F32),
        ],
        flops=20 * rows * every * dim,
    )
    from_cross, query_part = tie((from_cross, query_part))
    from_prompt, pay6, pay5 = call(
        return_kernel,
        [grads_wide, packed, packed],
        (facts, totals, near_sum, from_group, from_seq, from_cross),
    )
    far5 = along_grp(pay5, 5)
    far6 = along_grp(pay6, 6)
    own_back = along_seq(own_back, 1)
    rest = along_grp(totals, 2)
    query_grad, key_grad, value_grad, loss = call(
        finish_kernel,
        [
            shape((rows, width), BF16),
            shape((rows, dim), BF16),
            shape((rows, dim), BF16),
            shape((1, group_count // 2), F32),
        ],
        (facts, local, own_back, from_prompt, far5, far6, totals, rest, query_part),
    )
    return attended[None], query_grad[None], key_grad[None], value_grad[None], loss[0]


def solution(mesh):
    spec = P("grp", "seq", "head")
    in_specs = (spec, spec, spec, spec, P("grp", "seq"), P("grp", ("seq", "head")), P(), P())
    out_specs = (spec, spec, spec, spec, P())
    return jax.shard_map(body, mesh=mesh, in_specs=in_specs, out_specs=out_specs, check_vma=False)
```

```python
import functools
import math

import jax
import jax.numpy as jnp
from jax import lax
from jax.experimental import pallas as pl
from jax.experimental.pallas import tpu as pltpu
from jax.sharding import PartitionSpec as P

LEN_BLOCK = 128
BETA = 0.1
NEG_FILL = -1e30
LOG2_E = math.log2(math.e)
TAIL = 16
F32 = jnp.float32
BF16 = jnp.bfloat16
VMEM_BYTES = 40 * 1024 * 1024

VMEM_SPEC = pl.BlockSpec(memory_space=pltpu.VMEM)
HBM_SPEC = pl.BlockSpec(memory_space=pltpu.HBM)

FROM6, FROM5, IS_PROMPT, VALID, PAIR_ROW = 0, 4, 8, 9, 10
BIAS_FIRST, BIAS_MATE, BIAS_OVER, BIAS_CROSS, BIAS_OWN = 11, 12, 13, 14, 15
FACTS = 16


def dot(lhs, rhs, lhs_dim, rhs_dim):
    return lax.dot_general(
        lhs, rhs, (((lhs_dim,), (rhs_dim,)), ((), ())), preferred_element_type=F32
    )


def fact(facts_ref, row, width=None):
    return facts_ref[row : row + 1, :width]


def store_tail(ref, row, totals):
    high = totals.astype(BF16).astype(F32)
    rest = totals - high
    middle = rest.astype(BF16).astype(F32)
    low = rest - middle
    zero = jnp.zeros_like(middle)
    ref[row : row + TAIL, :128] = jnp.concatenate([high, low], axis=0).astype(BF16)
    ref[row : row + TAIL, 128:] = jnp.concatenate([middle, zero], axis=0).astype(BF16)


def decode(ref, row):
    left = ref[row : row + TAIL, :128].astype(F32)
    right = ref[row : row + TAIL, 128:].astype(F32)
    return (left[:8] + right[:8]) + left[8:]


def facts_kernel(
    order_hbm,
    counts_hbm,
    mask_hbm,
    ratio_hbm,
    key_hbm,
    value_hbm,
    own_ref,
    facts_ref,
    totals_ref,
    kept_ref,
    order_ref,
    counts_ref,
    mask_ref,
    ratio_ref,
    sems,
):
    dim = key_hbm.shape[1]
    copies = [
        pltpu.make_async_copy(source, target, sems.at[i])
        for i, (source, target) in enumerate(
            (
                (order_hbm, order_ref),
                (counts_hbm, counts_ref),
                (mask_hbm, mask_ref),
                (ratio_hbm, ratio_ref),
                (key_hbm, own_ref.at[:, pl.ds(0, dim)]),
                (value_hbm, own_ref.at[:, pl.ds(dim, dim)]),
            )
        )
    ]
    for copy in copies:
        copy.start()
    seq = lax.axis_index("seq")
    grp = lax.axis_index("grp")
    head = lax.axis_index("head")
    pairs = lax.axis_size("grp") // 2
    is_response = grp >= pairs
    for copy in copies[:4]:
        copy.wait()

    def pair_of(group, half):
        return order_ref[jnp.where(is_response, 2 * (group - pairs), 0) + half] // 2

    def put(row, value):
        facts_ref[row : row + 1, :] = jnp.full((1, facts_ref.shape[1]), value, F32)

    def flag(row, condition, yes=1.0, no=0.0):
        put(row, jnp.where(condition, yes, no).astype(F32))

    half = seq // 2
    slots = [pair_of(group, side) for side in (half, 1 - half) for group in (grp, grp ^ 1)]
    for number, pair in enumerate(slots):
        flag(FROM6 + number, jnp.logical_and(is_response, pair == (grp ^ 6)))
        flag(FROM5 + number, jnp.logical_and(is_response, pair == (grp ^ 5)))
    slot = jnp.where(is_response, 2 * (grp - pairs), 0) + half
    filled = seq % 2 < counts_ref[slot]
    valid = jnp.logical_or(jnp.logical_not(is_response), filled)
    my_pair = jnp.where(is_response, order_ref[slot] // 2, jnp.minimum(grp, pairs - 1))
    flag(IS_PROMPT, jnp.logical_not(is_response))
    flag(VALID, valid)
    put(PAIR_ROW, (2 * my_pair).astype(F32))
    flag(BIAS_FIRST, is_response, 0.0, NEG_FILL)
    flag(BIAS_MATE, jnp.logical_or(is_response, seq % 2 == 1), 0.0, NEG_FILL)
    flag(BIAS_OVER, jnp.logical_or(is_response, seq >= 2), 0.0, NEG_FILL)
    flag(BIAS_CROSS, jnp.logical_or(is_response, seq >= 2), 0.0, NEG_FILL)
    flag(BIAS_OWN, jnp.logical_and(is_response, seq % 2 == 1), 0.0, NEG_FILL)

    piece = ratio_ref.shape[1]
    lane = lax.broadcasted_iota(jnp.int32, (piece, 128), 1)
    spot = lax.broadcasted_iota(jnp.int32, (piece, 128), 0)
    place_at = (lane == spot + head * piece).astype(F32)
    spread = lax.dot_general(
        jnp.broadcast_to(ratio_ref[...], (8, piece)),
        place_at,
        (((1,), (0,)), ((), ())),
        precision=lax.Precision.HIGHEST,
        preferred_element_type=F32,
    )
    kept = mask_ref[...] > 0
    partial = jnp.sum(jnp.where(kept, spread[:1], 0.0), axis=1, keepdims=True)
    row = lax.broadcasted_iota(jnp.int32, (8, 128), 0)
    mine = jnp.where(jnp.logical_and(is_response, filled), order_ref[slot], -1)
    totals_ref[...] = jnp.where(row == mine, jnp.broadcast_to(partial, (8, 128)), 0.0)
    negative = jnp.logical_and(is_response, order_ref[slot] % 2 == 0)
    sign = jnp.where(valid, jnp.where(negative, -1.0, 1.0), 0.0).astype(F32)
    kept_ref[...] = jnp.where(kept, sign, 0.0)
    for copy in copies[4:]:
        copy.wait()


def prepare_kernel(
    kept_ref, query_hbm, cot_hbm, query_ref, query_t_ref, grad_ref, grad_t_ref, cots, sems
):
    rows = kept_ref.shape[1]
    dim = query_ref.shape[1]
    heads = query_ref.shape[0] // rows
    copies = []
    for i in range(heads):
        for j, (source, target) in enumerate(((cot_hbm, cots), (query_hbm, query_ref))):
            copies.append(
                pltpu.make_async_copy(
                    source.at[:, pl.ds(i * dim, dim)],
                    target.at[pl.ds(i * rows, rows)],
                    sems.at[j, i],
                )
            )
    for copy in copies:
        copy.start()
    kept_rows = jnp.broadcast_to(kept_ref[...], (rows, rows)).T
    for copy in copies:
        copy.wait()
    for i in range(heads):
        part = slice(i * rows, (i + 1) * rows)
        grad = (cots[part].astype(F32) * kept_rows).astype(BF16)
        grad_ref[part] = grad
        grad_t_ref[:, part] = grad.T
        query_t_ref[:, part] = query_ref[part].T


def route_kernel(facts_ref, totals_ref, own_ref, far6, far5, group_ref, seq_ref, cross_ref):
    rows = own_ref.shape[0]
    for number, ref in ((1, group_ref), (2, seq_ref), (3, cross_ref)):
        picked = far6[...].astype(F32) * fact(facts_ref, FROM6 + number)
        picked = picked + far5[...].astype(F32) * fact(facts_ref, FROM5 + number)
        if number == 2:
            picked = picked + own_ref[...].astype(F32) * fact(facts_ref, IS_PROMPT)
        ref[:rows] = picked.astype(BF16)
        store_tail(ref, rows, totals_ref[...])


def select_kernel(
    facts_ref, totals_ref, own_ref, far6, far5, group_ref, seq_ref, cross_ref, near_ref, sum_ref
):
    rows = own_ref.shape[0]
    first = far6[...].astype(F32) * fact(facts_ref, FROM6)
    first = first + far5[...].astype(F32) * fact(facts_ref, FROM5)
    first = first + own_ref[...].astype(F32) * fact(facts_ref, IS_PROMPT)
    near_ref[:rows] = (first + group_ref[:rows].astype(F32)).astype(BF16)
    near_ref[rows:] = (seq_ref[:rows].astype(F32) + cross_ref[:rows].astype(F32)).astype(BF16)
    totals = (totals_ref[...] + decode(group_ref, rows)) + (
        decode(seq_ref, rows) + decode(cross_ref, rows)
    )
    sum_ref[...] = jnp.concatenate([totals] * (sum_ref.shape[0] // 8), axis=0)


def load_blocks(blocks, keys, values, keys_t, values_t):
    dim = keys.shape[1]
    rows = keys.shape[0] // len(blocks)
    for number, (ref, start) in enumerate(blocks):
        part = slice(number * rows, (number + 1) * rows)
        key_part = ref[start : start + rows, :dim]
        value_part = ref[start : start + rows, dim:]
        keys[part] = key_part
        values[part] = value_part
        keys_t[:, part] = key_part.T
        values_t[:, part] = value_part.T


def early_kernel(
    biases,
    is_own,
    facts_ref,
    query_ref,
    grad_ref,
    left_ref,
    right_ref,
    powers_ref,
    prob_grad_ref,
    stats_ref,
    keys_t,
    values_t,
    keys,
    values,
):
    rows = keys.shape[0] // 2
    heads = query_ref.shape[0] // rows
    shade = LOG2_E / math.sqrt(keys.shape[1])
    start = 0 if is_own else rows
    load_blocks(((left_ref, 0), (right_ref, start)), keys, values, keys_t, values_t)
    wide = 2 * rows
    key_id = lax.broadcasted_iota(jnp.int32, (rows, wide), 0)
    row_id = lax.broadcasted_iota(jnp.int32, (rows, wide), 1) % rows
    causal = key_id <= row_id
    bias = [fact(facts_ref, row, wide) if row is not None else 0.0 for row in biases]
    for pair in range(heads // 2):
        both = slice(pair * wide, (pair + 1) * wide)
        scores = dot(keys[...], query_ref[both], 1, 1)
        prob_grad_ref[:, both] = dot(values[...], grad_ref[both], 1, 1)
        pieces = [scores[:rows], scores[rows:]]
        if is_own:
            pieces[1] = jnp.where(causal, pieces[1], NEG_FILL)
        tops = [jnp.max(piece, axis=0, keepdims=True) for piece in pieces]
        top = jnp.maximum(tops[0] + bias[0], tops[1] + bias[1])
        total = jnp.zeros_like(top)
        for i, piece in enumerate(pieces):
            power = jnp.exp2(piece * shade + (bias[i] - shade * top))
            total = total + jnp.sum(power, axis=0, keepdims=True)
            powers_ref[i * rows : (i + 1) * rows, both] = power.astype(BF16)
        stats_ref[0:1, both] = top
        stats_ref[1:2, both] = total


def scaled(ref, scales_ref, row):
    return (ref[...].astype(F32) * scales_ref[row : row + 1, :]).astype(BF16)


def store_grads(ref, score_grad, powers, query_t, grad_t, scaling):
    dim = query_t.shape[0]
    ref[:, :dim] = (dot(score_grad, query_t, 1, 1) * scaling).astype(ref.dtype)
    ref[:, dim:] = dot(powers, grad_t, 1, 1).astype(ref.dtype)


def late_kernel(
    facts_ref,
    query_ref,
    query_t_ref,
    grad_ref,
    grad_t_ref,
    own_powers,
    own_stats,
    own_values_t,
    near_powers,
    near_stats,
    near_values_t,
    mate_ref,
    back_ref,
    output_t_ref,
    score_grad,
    keys_t,
    scales_ref,
    keys,
    values,
    values_t,
    powers,
    prob_grad,
    stats,
):
    rows, dim = keys.shape[0] // 2, keys.shape[1]
    heads = query_ref.shape[0] // rows
    scaling = 1.0 / math.sqrt(dim)
    shade = LOG2_E * scaling
    load_blocks(((mate_ref, 0), (mate_ref, rows)), keys, values, keys_t, values_t)
    wide = 2 * rows
    spans = [slice(pair * wide, (pair + 1) * wide) for pair in range(heads // 2)]
    bias = [fact(facts_ref, row, wide) for row in (BIAS_MATE, BIAS_CROSS)]
    for both in spans:
        scores = dot(keys[...], query_ref[both], 1, 1)
        prob_grad[:, both] = dot(values[...], grad_ref[both], 1, 1)
        pieces = [scores[:rows], scores[rows:]]
        tops = [jnp.max(pieces[i], axis=0, keepdims=True) + bias[i] for i in (0, 1)]
        top = jnp.maximum(tops[0], tops[1])
        total = jnp.zeros_like(top)
        for i, piece in enumerate(pieces):
            power = jnp.exp2(piece * shade + (bias[i] - shade * top))
            total = total + jnp.sum(power, axis=0, keepdims=True)
            powers[i * rows : (i + 1) * rows, both] = power.astype(BF16)
        stats[0:1, both] = top
        stats[1:2, both] = total

    sets = (
        (own_powers, own_stats, own_values_t),
        (near_powers, near_stats, near_values_t),
        (powers, stats, values_t),
    )
    tops = [item[1][0:1, :] for item in sets]
    top = jnp.maximum(jnp.maximum(tops[0], tops[1]), tops[2])
    fades = [jnp.exp2((part - top) * shade) for part in tops]
    total = sum(item[1][1:2, :] * fade for item, fade in zip(sets, fades))
    inverse = 1.0 / total
    for i, fade in enumerate(fades):
        scales_ref[i : i + 1, :] = fade * inverse
    for both in spans:
        output_t = sum(
            dot(item[2][...], item[0][:, both], 1, 0) * scales_ref[i : i + 1, both]
            for i, item in enumerate(sets)
        )
        output_t_ref[:, both] = output_t
        delta = jnp.sum(grad_t_ref[:, both].astype(F32) * output_t, axis=0, keepdims=True)
        scales_ref[3:4, both] = delta
        score_grad[:, both] = (
            powers[:, both].astype(F32) * (prob_grad[:, both] - delta)
        ).astype(BF16)
    store_grads(
        back_ref,
        score_grad[...],
        powers[...],
        scaled(query_t_ref, scales_ref, 2),
        scaled(grad_t_ref, scales_ref, 2),
        scaling,
    )


def near_kernel(
    query_t_ref, grad_t_ref, powers, prob_grad, scales_ref, near_ref, score_grad
):
    scaling = 1.0 / math.sqrt(query_t_ref.shape[0])
    delta = scales_ref[3:4, :]
    score_grad[...] = (powers[...].astype(F32) * (prob_grad[...] - delta)).astype(BF16)
    store_grads(
        near_ref,
        score_grad[...],
        powers[...],
        scaled(query_t_ref, scales_ref, 1),
        scaled(grad_t_ref, scales_ref, 1),
        scaling,
    )


def query_kernel(
    facts_ref,
    query_t_ref,
    grad_t_ref,
    output_t_ref,
    scales_ref,
    own_powers,
    own_prob_grad,
    near_score_grad,
    mate_score_grad,
    own_keys_t,
    near_keys_t,
    mate_keys_t,
    attended_ref,
    query_grad_ref,
    back_ref,
    local_ref,
    own_score_grad,
    grads_ref,
):
    rows = attended_ref.shape[0]
    dim = output_t_ref.shape[0]
    scaling = 1.0 / math.sqrt(dim)
    wide = 2 * rows
    valid = fact(facts_ref, VALID, wide)
    for pair in range(output_t_ref.shape[1] // wide):
        both = slice(pair * wide, (pair + 1) * wide)
        delta = scales_ref[3:4, both]
        own_score_grad[:, both] = (
            own_powers[:, both].astype(F32) * (own_prob_grad[:, both] - delta)
        ).astype(BF16)
        sets = (
            (own_keys_t, own_score_grad),
            (near_keys_t, near_score_grad),
            (mate_keys_t, mate_score_grad),
        )
        grad_t = sum(
            dot(part_t[...], part[:, both], 1, 0) * scales_ref[i : i + 1, both]
            for i, (part_t, part) in enumerate(sets)
        )
        query_grad = (grad_t * scaling).T
        output = (output_t_ref[:, both] * valid).T
        for i in (0, 1):
            span = slice((2 * pair + i) * dim, (2 * pair + i + 1) * dim)
            part = slice(i * rows, (i + 1) * rows)
            attended_ref[:, span] = output[part].astype(BF16)
            query_grad_ref[:, span] = query_grad[part]
    store_grads(
        grads_ref,
        own_score_grad[...],
        own_powers[...],
        scaled(query_t_ref, scales_ref, 0),
        scaled(grad_t_ref, scales_ref, 0),
        scaling,
    )
    back_ref[...] = grads_ref[:rows].astype(BF16)
    local_ref[...] = grads_ref[rows:]


def merge_kernel(first_ref, back_ref, near_out, over_out):
    rows = first_ref.shape[0] // 2
    near_out[...] = (first_ref[:rows] + back_ref[:rows].astype(F32)).astype(BF16)
    over_out[...] = (first_ref[rows:] + back_ref[rows:].astype(F32)).astype(BF16)


def return_kernel(
    facts_ref, totals_ref, near_ref, group_ref, seq_ref, cross_ref, prompt_ref, pay6, pay5
):
    rows = prompt_ref.shape[0]
    sums = [ref[...].astype(F32) for ref in (near_ref, group_ref, seq_ref, cross_ref)]
    prompt_ref[...] = (sums[0] + sums[2]) * fact(facts_ref, IS_PROMPT)
    for ref, base in ((pay6, FROM6), (pay5, FROM5)):
        total = sum(part * fact(facts_ref, base + i) for i, part in enumerate(sums))
        ref[:rows] = total.astype(BF16)
        store_tail(ref, rows, totals_ref[...])


def finish_kernel(
    facts_ref,
    local_ref,
    mate_ref,
    prompt_ref,
    far5,
    far6,
    totals_ref,
    rest_ref,
    query_part_ref,
    query_grad_ref,
    key_grad_ref,
    value_grad_ref,
    loss_ref,
):
    rows, dim = key_grad_ref.shape
    totals = (totals_ref[...] + rest_ref[...]) + (decode(far6, rows) + decode(far5, rows))
    margin = totals - jnp.concatenate([totals[1:], totals[:1]], axis=0)
    slope = -BETA * margin
    small = jnp.exp(-jnp.abs(slope))
    bigger = 1.0 + small
    gap = bigger - 1.0
    log_part = jnp.where(
        gap == 0.0, small, jnp.log(bigger) * (small / jnp.where(gap == 0.0, 1.0, gap))
    )
    loss = jnp.maximum(slope, 0.0) + log_part
    weight = jnp.where(slope >= 0.0, 1.0, small) / bigger
    row = lax.broadcasted_iota(jnp.int32, (8, 128), 0)
    lane = lax.broadcasted_iota(jnp.int32, (8, 128), 1)
    in_lanes = jnp.sum(jnp.where(row == 2 * lane, loss, 0.0), axis=0, keepdims=True)
    loss_ref[...] = in_lanes[:, : loss_ref.shape[1]]
    mine = row.astype(F32) == fact(facts_ref, PAIR_ROW, 128)
    scale = jnp.sum(jnp.where(mine, weight, 0.0), axis=0, keepdims=True)
    far_sum = far6[:rows].astype(F32) + far5[:rows].astype(F32)
    total = local_ref[...] + mate_ref[...].astype(F32) + prompt_ref[...]
    total = total + far_sum * fact(facts_ref, IS_PROMPT)
    key_grad_ref[...] = (total[:, :dim] * scale).astype(BF16)
    value_grad_ref[...] = (total[:, dim:] * scale).astype(BF16)
    for start in range(0, query_grad_ref.shape[1], dim):
        span = slice(start, start + dim)
        query_grad_ref[:, span] = (query_part_ref[:, span] * scale).astype(BF16)


def call(kernel, out_shapes, operands, scratch=(), in_hbm=0, flops=0):
    single = not isinstance(out_shapes, (list, tuple))
    plain = len(operands) - in_hbm
    held = [
        pltpu.with_memory_space_constraint(operand, pltpu.HBM) for operand in operands[plain:]
    ]
    return pl.pallas_call(
        kernel,
        out_shape=out_shapes,
        in_specs=[VMEM_SPEC] * plain + [HBM_SPEC] * in_hbm,
        out_specs=VMEM_SPEC if single else [VMEM_SPEC] * len(out_shapes),
        scratch_shapes=list(scratch),
        compiler_params=pltpu.CompilerParams(vmem_limit_bytes=VMEM_BYTES),
        cost_estimate=pl.CostEstimate(flops=flops, bytes_accessed=0, transcendentals=0),
    )(*operands[:plain], *held)


def swap(count, turn):
    return [(i, i ^ turn) for i in range(count)]


def body(
    queries, key_heads, value_heads, cotangent, loss_mask, log_ratio, block_counts, response_order
):
    seq_count = lax.axis_size("seq")
    group_count = lax.axis_size("grp")
    head_count = lax.axis_size("head")
    rows = queries.shape[1]
    dim = key_heads.shape[2]
    width = queries.shape[2]
    heads = width // dim
    both = 2 * dim
    every = heads * rows
    shape = jax.ShapeDtypeStruct
    dma = pltpu.SemaphoreType.DMA
    tie = lax.optimization_barrier
    packed = shape((rows + TAIL, both), BF16)
    total_tile = shape((8, 128), F32)
    grads = shape((rows, both), BF16)
    grads_wide = shape((rows, both), F32)

    def along_grp(value, turn):
        return lax.ppermute(value, "grp", swap(group_count, turn))

    def along_seq(value, turn):
        return lax.ppermute(value, "seq", swap(seq_count, turn))

    def across(value):
        turns = [
            (s * group_count + g, (s ^ 2) * group_count + (g ^ 1))
            for s in range(seq_count)
            for g in range(group_count)
        ]
        return lax.ppermute(value, ("seq", "grp"), turns)

    def along_x(value, step):
        near = [(h, h ^ 2) for h in range(head_count)]
        round_way = [(h, (3 - h // 2) * 2 + h % 2) for h in range(head_count)]
        return lax.ppermute(value, "head", round_way if step else near)

    def along_y(value):
        return lax.ppermute(value, "head", swap(head_count, 1))

    own, facts, totals, kept = call(
        facts_kernel,
        [grads, shape((FACTS, both), F32), total_tile, shape((1, rows), F32)],
        (
            response_order,
            block_counts,
            loss_mask,
            log_ratio,
            key_heads[0],
            value_heads[0],
        ),
        scratch=[
            pltpu.SMEM(response_order.shape, jnp.int32),
            pltpu.SMEM(block_counts.shape, jnp.int32),
            pltpu.VMEM(loss_mask.shape, jnp.int32),
            pltpu.VMEM(log_ratio.shape, F32),
            dma((6,)),
        ],
        in_hbm=6,
    )
    far6 = along_grp(own, 6)
    far5 = along_grp(own, 5)
    mate_own = along_seq(own, 1)
    stacked = shape((every, dim), BF16)
    query_rows, query_cols, grad_rows, grad_cols = call(
        prepare_kernel,
        [stacked, shape((dim, every), BF16), stacked, shape((dim, every), BF16)],
        (kept, queries[0], cotangent[0]),
        scratch=[pltpu.VMEM((every, dim), BF16), dma((2, heads))],
        in_hbm=2,
    )
    part = along_y(totals)
    far6, far5, totals, query_rows = tie((far6, far5, totals, query_rows))
    totals = totals + part
    far6, far5, totals = tie((far6, far5, totals))
    to_group, to_seq, to_cross = call(
        route_kernel, [packed] * 3, (facts, totals, own, far6, far5)
    )
    from_seq = along_seq(to_seq, 2)
    from_group = along_grp(to_group, 1)
    from_cross = across(to_cross)

    def early(biases, is_own, left, right):
        return call(
            functools.partial(early_kernel, biases, is_own),
            [
                shape((2 * rows, every), BF16),
                shape((2 * rows, every), F32),
                shape((8, every), F32),
                shape((dim, 2 * rows), BF16),
                shape((dim, 2 * rows), BF16),
            ],
            (facts, query_rows, grad_rows, left, right),
            scratch=[pltpu.VMEM((2 * rows, dim), BF16)] * 2,
            flops=8 * rows * every * dim,
        )

    own_set = early((BIAS_OWN, None), True, mate_own, own)
    from_cross, own_powers = tie((from_cross, own_set[0]))
    near, totals = call(
        select_kernel,
        [shape((2 * rows, both), BF16), shape((rows // 2, 128), F32)],
        (facts, totals, own, far6, far5, from_group, from_seq, from_cross),
    )
    mate = along_seq(near, 1)
    near_set = early((BIAS_FIRST, BIAS_OVER), False, near, near)
    part = along_seq(totals, 1)
    mate, near_powers = tie((mate, near_set[0]))
    back, output_t, mate_sg, mate_keys_t, scales = call(
        late_kernel,
        [
            shape((2 * rows, both), BF16),
            shape((dim, every), F32),
            shape((2 * rows, every), BF16),
            shape((dim, 2 * rows), BF16),
            shape((8, every), F32),
        ],
        (
            facts,
            query_rows,
            query_cols,
            grad_rows,
            grad_cols,
            own_powers,
            own_set[2],
            own_set[4],
            near_powers,
            near_set[2],
            near_set[4],
            mate,
        ),
        scratch=[
            pltpu.VMEM((2 * rows, dim), BF16),
            pltpu.VMEM((2 * rows, dim), BF16),
            pltpu.VMEM((dim, 2 * rows), BF16),
            pltpu.VMEM((2 * rows, every), BF16),
            pltpu.VMEM((2 * rows, every), F32),
            pltpu.VMEM((8, every), F32),
        ],
        flops=24 * rows * every * dim,
    )
    back, totals = tie((back, totals))
    back, totals = tie((back, totals + part))
    back = along_seq(back, 1)
    part = along_x(totals, 0)
    first, near_sg = call(
        near_kernel,
        [shape((2 * rows, both), F32), shape((2 * rows, every), BF16)],
        (query_cols, grad_cols, near_powers, near_set[1], scales),
        flops=8 * rows * every * dim,
    )
    near_sum, over_sum = call(merge_kernel, [grads, grads], (first, back))
    from_seq = along_seq(over_sum, 2)
    from_group = along_grp(near_sum, 1)
    from_cross = across(over_sum)
    totals = (totals + part)[:8]
    totals = totals + along_x(totals, 1)
    attended, query_part, own_back, local = call(
        query_kernel,
        [shape((rows, width), BF16), shape((rows, width), F32), grads, grads_wide],
        (
            facts,
            query_cols,
            grad_cols,
            output_t,
            scales,
            own_powers,
            own_set[1],
            near_sg,
            mate_sg,
            own_set[3],
            near_set[3],
            mate_keys_t,
        ),
        scratch=[
            pltpu.VMEM((2 * rows, every), BF16),
            pltpu.VMEM((2 * rows, both), F32),
        ],
        flops=20 * rows * every * dim,
    )
    from_cross, query_part = tie((from_cross, query_part))
    from_prompt, pay6, pay5 = call(
        return_kernel,
        [grads_wide, packed, packed],
        (facts, totals, near_sum, from_group, from_seq, from_cross),
    )
    far5 = along_grp(pay5, 5)
    far6 = along_grp(pay6, 6)
    own_back = along_seq(own_back, 1)
    rest = along_grp(totals, 2)
    query_grad, key_grad, value_grad, loss = call(
        finish_kernel,
        [
            shape((rows, width), BF16),
            shape((rows, dim), BF16),
            shape((rows, dim), BF16),
            shape((1, group_count // 2), F32),
        ],
        (facts, local, own_back, from_prompt, far5, far6, totals, rest, query_part),
    )
    return attended[None], query_grad[None], key_grad[None], value_grad[None], loss[0]


def solution(mesh):
    spec = P("grp", "seq", "head")
    in_specs = (spec, spec, spec, spec, P("grp", "seq"), P("grp", ("seq", "head")), P(), P())
    out_specs = (spec, spec, spec, spec, P())
    return jax.shard_map(body, mesh=mesh, in_specs=in_specs, out_specs=out_specs, check_vma=False)
```
